32 devices in a mesh: space: 4 (over y, x), dp: 8 (over z, core).
Axes of the slice: x: 2, y: 2, z: 4, core: 2. Of those that a mesh axis runs over, the one named last changes fastest.
Arguments:
- volumes: bfloat16 [8, 4, 32, 8, 128], P('dp', None, 'space'), may hold values from -6 to 6
- first_kernel: bfloat16 [16, 4, 3, 3, 3], replicated, may hold values from -1 to 1
- middle_kernel: bfloat16 [32, 16, 3, 3, 3], replicated, may hold values from -0.5 to 0.5
- cotangent: bfloat16 [8, 32, 8, 2, 32], P('dp', None, 'space'), may hold values from -48 to 48
Outputs:
- features: bfloat16 [8, 32, 8, 2, 32], P('dp', None, 'space')
- first_grad: float32 [16, 4, 3, 3, 3], replicated
- middle_grad: float32 [32, 16, 3, 3, 3], replicated
The draws below stay inside these ranges and needn't reach their ends.
All inputs are finite; a program needn't handle non-finite values.
Results may differ from the reference program's by a relative error of at most 0.007.
Values may be sent and summed in bfloat16 or wider, within the bound.
A program may use at most 64 MiB of HBM per device.

```python
import math
import jax
import jax.numpy as jnp
from jax import lax

C_IN = 4
C1 = 16
C2 = 32
VY = 8
VZ = 128
VX = 32
SAMPLES = 8


def block_levels(stream_key, dims, split, least, high):
    level, own = 1.0, jax.random.fold_in(stream_key, 6)
    for position, blocks in split:
        steps = jnp.exp(jax.random.uniform(jax.random.fold_in(own, position), (blocks,), jnp.float32, least / len(split), high / len(split)))
        level = level * jnp.repeat(steps, dims[position] // blocks).reshape([-1 if axis == position else 1 for axis in range(len(dims))])
    return level


def gaussian(key, extent, spread, reach, cuts=(), kind=jnp.bfloat16):
    values = jax.random.normal(key, extent, jnp.float32) * spread
    if len(cuts) > 0:
        values = block_levels(key, extent, cuts, -0.22, 0.18) * values
    return jnp.clip(values, min=-reach, max=reach).astype(kind)


def setup_inputs(seed: int = 0) -> dict:
    seeds = jax.random.split(jax.random.key(seed), 5)
    return {
        "volumes": gaussian(seeds[0], (SAMPLES, C_IN, VX, VY, VZ), 1.0, 6.0, ((0, 8), (2, 4))),
        "first_kernel": gaussian(seeds[1], (C1, C_IN, 3, 3, 3), (C_IN * 9) ** -0.5, 1.0),
        "middle_kernel": gaussian(seeds[2], (C2, C1, 3, 3, 3), (C1 * 9) ** -0.5, 0.5),
        "cotangent": gaussian(seeds[3], (SAMPLES, C2, VX // 4, VY // 4, VZ // 4), 8.0, 48.0, ((0, 8), (2, 4))),
    }


leak_slope = 0.3
soft_share = 0.7
log_two = math.log(2.0)

def activate(values):
    return leak_slope * values + soft_share * (jax.nn.softplus(values) - log_two)

def slope_of(values):
    return leak_slope + soft_share * jax.nn.sigmoid(values)

def pool_cells(values):
    lead = values.shape[:-3]
    size_x, size_y, size_z = values.shape[-3:]
    grouped = values.reshape(lead + (size_x // 2, 2, size_y // 2, 2, size_z // 2, 2))
    return grouped.mean(axis=(-5, -3, -1))

def spread_cells(values):
    lead = values.shape[:-3]
    size_x, size_y, size_z = values.shape[-3:]
    wide = values.astype(jnp.float32)[..., :, None, :, None, :, None]
    wide = jnp.broadcast_to(wide, lead + (size_x, 2, size_y, 2, size_z, 2))
    return wide.reshape(lead + (2 * size_x, 2 * size_y, 2 * size_z)) * 0.125

def conv_same(values, kernel):
    result = lax.conv_general_dilated(values[None].astype(jnp.float32), kernel.astype(jnp.float32), (1, 1, 1), ((1, 1), (1, 1), (1, 1)), dimension_numbers=('NCDHW', 'OIDHW', 'NCDHW'), precision=lax.Precision.HIGHEST)
    return result[0]

def turned(kernel):
    return jnp.flip(kernel, (2, 3, 4)).transpose(1, 0, 2, 3, 4)

def tap_grad(values, delta):
    padded = jnp.pad(values.astype(jnp.float32), ((0, 0), (1, 1), (1, 1), (1, 1)))
    delta_wide = delta.astype(jnp.float32)
    size_x, size_y, size_z = delta.shape[1:]
    pieces = []
    for offset_x in range(3):
        for offset_y in range(3):
            for offset_z in range(3):
                window = padded[:, offset_x:offset_x + size_x, offset_y:offset_y + size_y, offset_z:offset_z + size_z]
                pieces.append(jnp.einsum('oxyz,cxyz->oc', delta_wide, window, precision=lax.Precision.HIGHEST))
    stacked = jnp.stack(pieces, -1)
    return stacked.reshape(delta.shape[0], values.shape[0], 3, 3, 3)

def reference(volumes, first_kernel, middle_kernel, cotangent):

    def one_volume(totals, pair):
        volume, cot_volume = pair
        pre_first = conv_same(volume, first_kernel)
        act_first = pool_cells(activate(pre_first)).astype(jnp.bfloat16)
        pre_middle = conv_same(act_first, middle_kernel)
        features = pool_cells(activate(pre_middle)).astype(jnp.bfloat16)
        delta_middle = (slope_of(pre_middle) * spread_cells(cot_volume)).astype(jnp.bfloat16)
        back_first = conv_same(delta_middle, turned(middle_kernel)).astype(jnp.bfloat16)
        delta_first = (slope_of(pre_first) * spread_cells(back_first)).astype(jnp.bfloat16)
        grad_first = tap_grad(volume, delta_first)
        grad_middle = tap_grad(act_first, delta_middle)
        return ((totals[0] + grad_first, totals[1] + grad_middle), features)
    zeros = (jnp.zeros(first_kernel.shape, jnp.float32), jnp.zeros(middle_kernel.shape, jnp.float32))
    totals, features = lax.scan(one_volume, zeros, (volumes, cotangent))
    scale = 1.0 / SAMPLES
    return (features, totals[0] * scale, totals[1] * scale)
```

```python
import functools
import math

import jax
import jax.numpy as jnp
from jax import lax
from jax.experimental import pallas as pl
from jax.experimental.pallas import tpu as pltpu
from jax.sharding import PartitionSpec as P

leak_slope = 0.3
soft_share = 0.7
log_two = math.log(2.0)
reach = 5
f32, bf16 = jnp.float32, jnp.bfloat16


def activate(a):
    soft = jnp.maximum(a, 0.0) + jnp.log(1.0 + jnp.exp(-jnp.abs(a)))
    return leak_slope * a + soft_share * (soft - log_two)


def slope_of(a):
    return leak_slope + soft_share / (1.0 + jnp.exp(-a))


def dot(a, b):
    return jnp.dot(a, b, preferred_element_type=f32)


def dot_lanes(a, b):
    return lax.dot_general(a, b, (((1,), (1,)), ((), ())), preferred_element_type=f32)


def dot_wide(a, b):
    high = a.astype(bf16)
    low = (a - high.astype(f32)).astype(bf16)
    return dot(high, b) + dot(low, b)


def grid_of(rows, cols):
    return (
        lax.broadcasted_iota(jnp.int32, (rows, cols), 0),
        lax.broadcasted_iota(jnp.int32, (rows, cols), 1),
    )


def pick(where, value=1.0):
    return jnp.where(where, value, 0.0).astype(bf16)


def z_taps(a, width):
    place = lax.broadcasted_iota(jnp.int32, a.shape, 1) & (width - 1)
    before = jnp.where(place == 0, 0.0, pltpu.roll(a, 1, 1))
    after = jnp.where(place == width - 1, 0.0, pltpu.roll(a, 127, 1))
    return jnp.concatenate([before, a, after], axis=0).astype(bf16)


def between(a, b):
    place = lax.broadcasted_iota(jnp.int32, a.shape, 1)
    return jnp.where(place < 64, pltpu.roll(a, 64, 1), pltpu.roll(b, 64, 1))


def kernel(
    n_space, n_dp, part,
    vol_ref, w1_ref, w2_ref, cot_ref,
    feat_ref, g1_ref, g2_ref,
    vol_left, vol_right, cot_left, cot_right, pay, got, across, full,
    halo_send, halo_recv, rs_send, rs_recv, ex_send, ex_recv, ag_send, ag_recv,
):
    s, d = lax.axis_index("space"), lax.axis_index("dp")
    n_a, n_b = 2 * n_space, n_dp // 2
    a, b = 2 * s + lax.rem(d, 2), d // 2
    inner = s > 0
    outer = s < n_space - 1

    def in_a(step):
        t = lax.rem(a + step, n_a)
        return t, {"space": t // 2, "dp": 2 * b + lax.rem(t, 2)}

    def in_b(step):
        t = lax.rem(b + step, n_b)
        return t, {"space": s, "dp": 2 * t + lax.rem(d, 2)}

    for ref in (vol_left, vol_right, cot_left, cot_right):
        ref[...] = jnp.zeros_like(ref)
    barrier = pltpu.get_barrier_semaphore()
    for step in range(1, n_a):
        pl.semaphore_signal(barrier, inc=1, device_id=in_a(step)[1], device_id_type=pl.DeviceIdType.MESH)
    for step in range(1, n_b):
        pl.semaphore_signal(barrier, inc=1, device_id=in_b(step)[1], device_id_type=pl.DeviceIdType.MESH)

    lane = lax.broadcasted_iota(jnp.int32, (1, 128), 1)
    deep_y = 2 * (lane & 1) + (lane >> 6)
    ro, co = grid_of(32, 128)
    t2 = dot(w2_ref[...].reshape(27 * 16, 32), pick(ro == (co & 63) >> 1))
    ro, co = grid_of(16, 128)
    w1 = jnp.concatenate([w1_ref[k].astype(f32) for k in range(27)], axis=0).astype(bf16)
    t1 = dot(w1, pick(ro == (co & 15)))
    ro, co = grid_of(8, 128)
    near_y = 2 * ((co & 63) >> 4) + (co >> 6)
    taps_y = [jnp.where(ro == near_y + q - 1, 1.0, 0.0) for q in range(3)]

    def tap2(k):
        return t2[16 * k : 16 * k + 16]

    w1_rows, w2_rows, wb_cols = [], [], []
    for p in range(3):
        for r in range(3):
            for c in range(4):
                rows = [4 * (9 * p + 3 * q + r) + c for q in range(3)]
                w1_rows.append(sum(t1[k : k + 1] * taps_y[q] for q, k in enumerate(rows)))
            ks = [9 * p + 3 * q + r for q in range(3)]
            block = []
            for y in range(4):
                w2_rows.append(sum(jnp.where(deep_y == y + 1 - q, tap2(k), 0.0) for q, k in enumerate(ks)))
                block.append(sum(jnp.where(deep_y == y + q - 1, tap2(26 - k), 0.0) for q, k in enumerate(ks)))
            wb_cols.append(jnp.concatenate(block, axis=0))
    w1_wide = jnp.concatenate(w1_rows, axis=0).T.astype(bf16)
    w2_wide = jnp.concatenate(w2_rows, axis=0).T.astype(bf16)
    wb_wide = jnp.concatenate(wb_cols, axis=1).astype(bf16)

    pl.semaphore_wait(barrier, n_a - 1 + n_b - 1)
    right = {"space": jnp.minimum(s + 1, n_space - 1), "dp": d}
    left = {"space": jnp.maximum(s - 1, 0), "dp": d}

    def halo(src, dst, sem, to):
        return pltpu.make_async_remote_copy(
            src_ref=src, dst_ref=dst, send_sem=halo_send.at[sem], recv_sem=halo_recv.at[sem],
            device_id=to, device_id_type=pl.DeviceIdType.MESH,
        )

    size_x = vol_ref.shape[1]
    to_right = [halo(vol_ref.at[:, size_x - reach : size_x], vol_left, 0, right), halo(cot_ref, cot_left, 1, right)]
    to_left = [halo(vol_ref.at[:, 0:reach], vol_right, 2, left), halo(cot_ref, cot_right, 3, left)]

    @pl.when(outer)
    def _():
        for copy in to_right:
            copy.start()

    @pl.when(inner)
    def _():
        for copy in to_left:
            copy.start()

    @pl.when(outer)
    def _():
        for copy in to_right:
            copy.wait_send()
        for copy in to_left:
            copy.wait_recv()

    @pl.when(inner)
    def _():
        for copy in to_left:
            copy.wait_send()
        for copy in to_right:
            copy.wait_recv()

    slabs = [(vol_left, i) for i in range(reach)] + [(vol_ref, i) for i in range(size_x)]
    slabs += [(vol_right, i) for i in range(reach)]
    taps = [z_taps(ref[:, i].astype(f32).reshape(32, 128), 128) for ref, i in slabs]
    taps = jnp.concatenate(taps, axis=1)
    count = 128 * (len(slabs) - 2)
    cols1 = jnp.concatenate([taps[:, 128 * p : 128 * p + count] for p in range(3)], axis=0)
    pre1 = dot(w1_wide, cols1)
    act1 = activate(pre1)
    act1 = act1[:64] + act1[64:]
    pairs = []
    for j in range(4):
        four = [act1[:, 128 * (4 * j + i) : 128 * (4 * j + i + 1)] for i in range(4)]
        pairs.append(jnp.concatenate([four[0] + four[1], four[2] + four[3]], axis=1))
    ro, co = grid_of(256, 128)
    pool = pick((ro >> 7 == co >> 6) & ((ro & 127) >> 1 == (co & 63)), 0.125)
    acts = dot_wide(jnp.concatenate(pairs, axis=0), pool).astype(bf16).astype(f32)
    even = [acts[64 * j : 64 * j + 64] for j in range(4)]
    even[0] = jnp.where(inner, even[0], 0.0)
    even[3] = jnp.where(outer, even[3], 0.0)
    odd = [between(even[j], even[j + 1]) for j in range(3)]

    even_taps = [z_taps(x, 64) for x in even]
    odd_taps = [z_taps(x, 64) for x in odd]
    cols2 = jnp.concatenate(
        [jnp.concatenate([even_taps[j], odd_taps[j], even_taps[j + 1]], axis=0) for j in range(3)], axis=1
    )
    pre2 = dot(w2_wide, cols2)
    act2 = activate(pre2)
    ro, co = grid_of(384, 64)
    row = ro >> 6
    pool = (row >= 1) & (row <= 4) & ((row - 1) >> 1 == co >> 5) & ((ro & 63) >> 1 == (co & 31))
    feat_ref[...] = dot_wide(act2[:64] + act2[64:], pick(pool, 0.125)).astype(bf16)

    ro, co = grid_of(64, 384)
    row = co >> 6
    same = (ro & 31) == (co & 63) >> 1
    wide = dot(cot_ref[...], pick(same & (row >= 1) & (row <= 4) & ((row - 1) >> 1 == ro >> 5), 0.125))
    wide += dot(cot_left[...], pick(same & (row == 0) & (ro >> 5 == 1), 0.125))
    wide += dot(cot_right[...], pick(same & (row == 5) & (ro >> 5 == 0), 0.125))
    delta2 = (slope_of(pre2) * jnp.concatenate([wide, wide], axis=0)).astype(bf16).astype(f32)
    row = lax.broadcasted_iota(jnp.int32, (128, 384), 1) >> 6
    own2 = jnp.where((row >= 1) & (row <= 4), delta2, 0.0).astype(bf16)

    odd = [delta2[:, 128 * j : 128 * j + 128] for j in range(3)]
    odd_taps = [z_taps(x, 64) for x in odd]
    even_taps = [z_taps(between(odd[j], odd[j + 1]), 64) for j in range(2)]
    cols3 = jnp.concatenate(
        [jnp.concatenate([odd_taps[j], even_taps[j], odd_taps[j + 1]], axis=0) for j in range(2)], axis=1
    )
    back = dot(wb_wide, cols3).astype(bf16)
    ro, co = grid_of(128, 256)
    spread = pick((ro >> 6 == co >> 7) & ((ro & 63) == (co & 127) >> 1), 0.125)
    wide = dot(jnp.concatenate([back[:, :128], back[:, 128:]], axis=0), spread)
    rows = [wide[64 * (i // 2) : 64 * (i // 2) + 64, 128 * (i % 2) : 128 * (i % 2) + 128] for i in range(4)]
    wide = jnp.concatenate([rows[i // 2] for i in range(8)], axis=1)
    first = 128 * (reach - 1)
    own = slice(first, first + 128 * size_x)
    delta1 = (slope_of(pre1[:, own]) * jnp.concatenate([wide, wide], axis=0)).astype(bf16)

    grad2 = dot_lanes(cols2, own2)
    blocks = []
    for k in range(27):
        p, q, r = k // 9, k // 3 % 3, k % 3
        at = 64 * (3 * p + r)
        blocks.append(
            sum(jnp.where(deep_y == y + 1 - q, grad2[at + 16 * y : at + 16 * y + 16], 0.0) for y in range(4))
        )
    blocks.append(jnp.zeros((16, 128), f32))
    groups = [jnp.concatenate(blocks[7 * j : 7 * j + 7], axis=0) for j in range(4)]
    ro, co = grid_of(512, 128)
    gather = pick((ro >> 7 == co >> 5) & ((ro & 63) >> 1 == (co & 31)))
    pay[0:112] = dot_wide(jnp.concatenate(groups, axis=1), gather)

    grad1 = dot_lanes(cols1[:, own], delta1).reshape(36, 8, 128)
    groups = [jnp.sum(grad1 * taps_y[q][None], axis=1) for q in range(3)]
    groups = jnp.concatenate([jnp.concatenate(groups, axis=1), jnp.zeros((4, 384), f32)], axis=0)
    ro, co = grid_of(384, 128)
    gather = pick((ro >> 7 == co >> 4) & ((ro & 15) == (co & 15)))
    pay[112:152] = dot_wide(groups, gather)
    if n_a * part > 152:
        pay[152:] = jnp.zeros((n_a * part - 152, 128), f32)

    def rows_of(t):
        return pl.ds(pl.multiple_of(t * part, 8), part)

    copies = []
    for step in range(1, n_a):
        t, to = in_a(step)
        copies.append(pltpu.make_async_remote_copy(
            src_ref=pay.at[rows_of(t)], dst_ref=got.at[step - 1],
            send_sem=rs_send.at[step - 1], recv_sem=rs_recv.at[step - 1],
            device_id=to, device_id_type=pl.DeviceIdType.MESH,
        ))
        copies[-1].start()
    total = pay[rows_of(a)]
    for i, copy in enumerate(copies):
        copy.wait_recv()
        total += got[i]
    for copy in copies:
        copy.wait_send()

    across[b] = total
    copies = []
    for step in range(1, n_b):
        t, to = in_b(step)
        copies.append(pltpu.make_async_remote_copy(
            src_ref=across.at[b], dst_ref=across.at[b],
            send_sem=ex_send.at[step - 1], recv_sem=ex_recv.at[step - 1],
            device_id=to, device_id_type=pl.DeviceIdType.MESH,
        ))
        copies[-1].start()
    for copy in copies:
        copy.wait()
    total = across[0]
    for i in range(1, n_b):
        total += across[i]

    full[rows_of(a)] = total * (1.0 / n_dp)
    copies = []
    for step in range(1, n_a):
        t, to = in_a(step)
        copies.append(pltpu.make_async_remote_copy(
            src_ref=full.at[rows_of(a)], dst_ref=full.at[rows_of(a)],
            send_sem=ag_send.at[step - 1], recv_sem=ag_recv.at[step - 1],
            device_id=to, device_id_type=pl.DeviceIdType.MESH,
        ))
        copies[-1].start()
    for copy in copies:
        copy.wait()

    for j in range(4):
        many = 7 if j < 3 else 6
        g2_ref[7 * j : 7 * j + many] = full[0 : 16 * many, 32 * j : 32 * j + 32].reshape(many, 16, 32)
    for k in range(27):
        p, q, r = k // 9, k // 3 % 3, k % 3
        at = 112 + 4 * (3 * p + r)
        g1_ref[k] = full[at : at + 4, 16 * q : 16 * q + 16]


def shards(n_space, n_dp, volumes, first_kernel, middle_kernel, cotangent):
    n_a, n_b = 2 * n_space, n_dp // 2
    part = 8 * -(-152 // (8 * n_a))
    w1 = first_kernel.transpose(2, 3, 4, 1, 0).reshape(27, 4, 16)
    w2 = middle_kernel.transpose(2, 3, 4, 1, 0).reshape(27, 16, 32)
    cot = cotangent[0].transpose(0, 2, 1, 3).reshape(64, 64)
    vol = volumes[0]
    halo = (vol.shape[0], reach) + vol.shape[2:]
    vmem = pl.BlockSpec(memory_space=pltpu.VMEM)
    dma = pltpu.SemaphoreType.DMA
    feat, g1, g2 = pl.pallas_call(
        functools.partial(kernel, n_space, n_dp, part),
        out_shape=(
            jax.ShapeDtypeStruct((64, 64), bf16),
            jax.ShapeDtypeStruct((27, 4, 16), f32),
            jax.ShapeDtypeStruct((27, 16, 32), f32),
        ),
        in_specs=[vmem] * 4,
        out_specs=(vmem, vmem, vmem),
        scratch_shapes=[
            pltpu.VMEM(halo, bf16),
            pltpu.VMEM(halo, bf16),
            pltpu.VMEM((64, 64), bf16),
            pltpu.VMEM((64, 64), bf16),
            pltpu.VMEM((n_a * part, 128), f32),
            pltpu.VMEM((n_a - 1, part, 128), f32),
            pltpu.VMEM((n_b, part, 128), f32),
            pltpu.VMEM((n_a * part, 128), f32),
            dma((4,)), dma((4,)),
            dma((n_a - 1,)), dma((n_a - 1,)),
            dma((max(n_b - 1, 1),)), dma((max(n_b - 1, 1),)),
            dma((n_a - 1,)), dma((n_a - 1,)),
        ],
        compiler_params=pltpu.CompilerParams(
            collective_id=0, has_side_effects=True, vmem_limit_bytes=48 * 1024 * 1024
        ),
        cost_estimate=pl.CostEstimate(flops=400_000_000, bytes_accessed=400_000, transcendentals=1_000_000),
    )(vol, w1, w2, cot)
    features = feat.reshape(32, 2, 2, 32).transpose(0, 2, 1, 3)[None]
    first_grad = g1.reshape(3, 3, 3, 4, 16).transpose(4, 3, 0, 1, 2)
    middle_grad = g2.reshape(3, 3, 3, 16, 32).transpose(4, 3, 0, 1, 2)
    return (features, first_grad, middle_grad)


def solution(mesh):
    in_specs = (P("dp", None, "space", None, None), P(), P(), P("dp", None, "space", None, None))
    out_specs = (P("dp", None, "space", None, None), P(), P())
    body = functools.partial(shards, mesh.shape["space"], mesh.shape["dp"])
    return jax.shard_map(body, mesh=mesh, in_specs=in_specs, out_specs=out_specs, check_vma=False)
```

```python
import functools
import math

import jax
import jax.numpy as jnp
from jax import lax
from jax.experimental import pallas as pl
from jax.experimental.pallas import tpu as pltpu
from jax.sharding import PartitionSpec as P

leak_slope = 0.3
soft_share = 0.7
log_two = math.log(2.0)
reach = 5
f32, bf16 = jnp.float32, jnp.bfloat16


def activate(a):
    soft = jnp.maximum(a, 0.0) + jnp.log(1.0 + jnp.exp(-jnp.abs(a)))
    return leak_slope * a + soft_share * (soft - log_two)


def activate_both(a):
    small = jnp.exp(-jnp.abs(a))
    whole = 1.0 + small
    soft = jnp.maximum(a, 0.0) + jnp.log(whole)
    act = leak_slope * a + soft_share * (soft - log_two)
    return act, leak_slope + soft_share * (jnp.where(a >= 0.0, 1.0, small) / whole)


def dot(a, b):
    return jnp.dot(a, b, preferred_element_type=f32)


def dot_lanes(a, b):
    return lax.dot_general(a, b, (((1,), (1,)), ((), ())), preferred_element_type=f32)


def dot_wide(a, b):
    high = a.astype(bf16)
    low = (a - high.astype(f32)).astype(bf16)
    return dot(high, b) + dot(low, b)


def grid_of(rows, cols):
    return (
        lax.broadcasted_iota(jnp.int32, (rows, cols), 0),
        lax.broadcasted_iota(jnp.int32, (rows, cols), 1),
    )


def pick(where, value=1.0):
    return jnp.where(where, value, 0.0).astype(bf16)


def z_taps(a, width):
    place = lax.broadcasted_iota(jnp.int32, a.shape, 1) & (width - 1)
    before = jnp.where(place == 0, 0.0, pltpu.roll(a, 1, 1))
    after = jnp.where(place == width - 1, 0.0, pltpu.roll(a, 127, 1))
    return jnp.concatenate([before, a, after], axis=0).astype(bf16)


def between(a, b):
    place = lax.broadcasted_iota(jnp.int32, a.shape, 1)
    return jnp.where(place < 64, pltpu.roll(a, 64, 1), pltpu.roll(b, 64, 1))


def remote(src, dst, send, recv, to):
    return pltpu.make_async_remote_copy(
        src_ref=src, dst_ref=dst, send_sem=send, recv_sem=recv, device_id=to, device_id_type=pl.DeviceIdType.MESH
    )


def kernel(
    n_space, n_dp, part,
    vol_hbm, w1_hbm, w2_hbm, cot_hbm,
    feat_ref, sums_ref,
    vol_ref, w1_ref, w2_ref, cot_ref, vol_left, vol_right, cot_left, cot_right, pay, got, across, full,
    pool1, pool2, spread1, spread2, gather1, gather2,
    load, halo_send, halo_recv, rs_send, rs_recv, ex_send, ex_recv, ag_send, ag_recv,
):
    s, d = lax.axis_index("space"), lax.axis_index("dp")
    n_a, n_b = 2 * n_space, n_dp // 2
    a, b = 2 * s + lax.rem(d, 2), d // 2
    inner = s > 0
    outer = s < n_space - 1

    def in_a(step):
        t = lax.rem(a + step, n_a)
        return t, {"space": t // 2, "dp": 2 * b + lax.rem(t, 2)}

    def in_b(step):
        t = lax.rem(b + step, n_b)
        return t, {"space": s, "dp": 2 * t + lax.rem(d, 2)}

    loads = [
        pltpu.make_async_copy(src, dst, load.at[i])
        for i, (src, dst) in enumerate(
            [(w2_hbm, w2_ref), (w1_hbm, w1_ref), (vol_hbm, vol_ref), (cot_hbm, cot_ref)]
        )
    ]
    for copy in loads:
        copy.start()
    for ref in (vol_left, vol_right, cot_left, cot_right):
        ref[...] = jnp.zeros_like(ref)
    barrier = pltpu.get_barrier_semaphore()
    for step in range(1, n_a):
        pl.semaphore_signal(barrier, inc=1, device_id=in_a(step)[1], device_id_type=pl.DeviceIdType.MESH)
    for step in range(1, n_b):
        pl.semaphore_signal(barrier, inc=1, device_id=in_b(step)[1], device_id_type=pl.DeviceIdType.MESH)
    pl.semaphore_wait(barrier, n_a - 1 + n_b - 1)

    right = {"space": jnp.minimum(s + 1, n_space - 1), "dp": d}
    left = {"space": jnp.maximum(s - 1, 0), "dp": d}
    size_x = vol_hbm.shape[1]
    deep_x = cot_hbm.shape[1]

    def halo(src, dst, sem, to):
        return remote(src, dst, halo_send.at[sem], halo_recv.at[sem], to)

    to_right = [
        halo(vol_hbm.at[:, size_x - reach : size_x], vol_left, 0, right),
        halo(cot_hbm.at[:, deep_x - 1], cot_left, 1, right),
    ]
    to_left = [halo(vol_hbm.at[:, 0:reach], vol_right, 2, left), halo(cot_hbm.at[:, 0], cot_right, 3, left)]

    @pl.when(outer)
    def _():
        for copy in to_right:
            copy.start()

    @pl.when(inner)
    def _():
        for copy in to_left:
            copy.start()

    lane = lax.broadcasted_iota(jnp.int32, (1, 128), 1)
    deep_y = 2 * (lane & 1) + (lane >> 6)
    ro, co = grid_of(32, 128)
    loads[0].wait()
    t2 = dot(w2_ref[...].reshape(27 * 16, 32), pick(ro == (co & 63) >> 1))
    ro, co = grid_of(16, 128)
    loads[1].wait()
    w1 = jnp.concatenate([w1_ref[k].astype(f32) for k in range(27)], axis=0).astype(bf16)
    t1 = dot(w1, pick(ro == (co & 15)))
    ro, co = grid_of(8, 128)
    near_y = 2 * ((co & 63) >> 4) + (co >> 6)
    taps_y = [jnp.where(ro == near_y + q - 1, 1.0, 0.0) for q in range(3)]

    def tap2(k):
        return t2[16 * k : 16 * k + 16]

    w1_rows, w2_rows, wb_cols = [], [], []
    for p in range(3):
        for r in range(3):
            for c in range(4):
                rows = [4 * (9 * p + 3 * q + r) + c for q in range(3)]
                w1_rows.append(sum(t1[k : k + 1] * taps_y[q] for q, k in enumerate(rows)))
            ks = [9 * p + 3 * q + r for q in range(3)]
            block = []
            for y in range(4):
                w2_rows.append(sum(jnp.where(deep_y == y + 1 - q, tap2(k), 0.0) for q, k in enumerate(ks)))
                block.append(sum(jnp.where(deep_y == y + q - 1, tap2(26 - k), 0.0) for q, k in enumerate(ks)))
            wb_cols.append(jnp.concatenate(block, axis=0))
    w1_wide = jnp.concatenate(w1_rows, axis=0).T.astype(bf16)
    w2_wide = jnp.concatenate(w2_rows, axis=0).T.astype(bf16)
    wb_wide = jnp.concatenate(wb_cols, axis=1).astype(bf16)

    def taps_of(ref, i):
        return z_taps(ref[:, i].astype(f32).reshape(32, 128), 128)

    def first_cols(taps):
        count = len(taps) - 2
        return jnp.concatenate([jnp.concatenate(taps[p : p + count], axis=1) for p in range(3)], axis=0)

    loads[2].wait()
    taps_own = [taps_of(vol_ref, i) for i in range(size_x)]
    cols_mid = first_cols(taps_own)
    act_mid, slope_mid = activate_both(dot(w1_wide, cols_mid))
    act_mid = act_mid[:64] + act_mid[64:]

    ro, co = grid_of(256, 128)
    pool1[...] = pick((ro >> 7 == co >> 6) & ((ro & 127) >> 1 == (co & 63)), 0.125)
    ro, co = grid_of(384, 64)
    row = ro >> 6
    same = (row >= 1) & (row <= 4) & ((row - 1) >> 1 == co >> 5) & ((ro & 63) >> 1 == (co & 31))
    pool2[...] = pick(same, 0.125)
    ro, co = grid_of(128, 384)
    spread2[...] = pick((((co >> 6) + 1) >> 1 == ro >> 5) & ((co & 63) >> 1 == (ro & 31)), 0.125)
    ro, co = grid_of(128, 256)
    spread1[...] = pick((ro >> 6 == co >> 7) & ((ro & 63) == (co & 127) >> 1), 0.125)
    ro, co = grid_of(512, 128)
    gather2[...] = pick((ro >> 7 == co >> 5) & ((ro & 63) >> 1 == (co & 31)))
    ro, co = grid_of(384, 128)
    gather1[...] = pick((ro >> 7 == co >> 4) & ((ro & 15) == (co & 15)))

    loads[3].wait()

    @pl.when(outer)
    def _():
        for copy in to_right:
            copy.wait_send()
        for copy in to_left:
            copy.wait_recv()

    @pl.when(inner)
    def _():
        for copy in to_left:
            copy.wait_send()
        for copy in to_right:
            copy.wait_recv()

    taps_low = [taps_of(vol_left, i) for i in range(reach)] + taps_own[:2]
    taps_high = taps_own[-2:] + [taps_of(vol_right, i) for i in range(reach)]
    cols_low, cols_high = first_cols(taps_low), first_cols(taps_high)
    edge = 128 * (reach - 1)
    pre_low, pre_high = dot(w1_wide, cols_low), dot(w1_wide, cols_high)
    act_low, act_high = activate(pre_low[:, :edge]), activate(pre_high[:, 128:])
    act_first, slope_first = activate_both(pre_low[:, edge:])
    act_last, slope_last = activate_both(pre_high[:, :128])
    act1 = [act_low, act_first, None, act_last, act_high]
    act1 = [act_mid if x is None else x[:64] + x[64:] for x in act1]
    act1 = jnp.concatenate(act1, axis=1)
    slope1 = jnp.concatenate([slope_first, slope_mid, slope_last], axis=1)
    cols1 = jnp.concatenate([cols_low[:, edge:], cols_mid, cols_high[:, :128]], axis=1)
    pairs = []
    for j in range(4):
        four = [act1[:, 128 * (4 * j + i) : 128 * (4 * j + i + 1)] for i in range(4)]
        pairs.append(jnp.concatenate([four[0] + four[1], four[2] + four[3]], axis=1))
    acts = dot_wide(jnp.concatenate(pairs, axis=0), pool1[...]).astype(bf16).astype(f32)
    even = [acts[64 * j : 64 * j + 64] for j in range(4)]
    even[0] = jnp.where(inner, even[0], 0.0)
    even[3] = jnp.where(outer, even[3], 0.0)
    odd = [between(even[j], even[j + 1]) for j in range(3)]

    even_taps = [z_taps(x, 64) for x in even]
    odd_taps = [z_taps(x, 64) for x in odd]
    cols2 = jnp.concatenate(
        [jnp.concatenate([even_taps[j], odd_taps[j], even_taps[j + 1]], axis=0) for j in range(3)], axis=1
    )
    act2, slope2 = activate_both(dot(w2_wide, cols2))

    def cot_rows(values):
        return values.astype(f32).reshape(64, 32)

    cots = [cot_left[...], cot_ref[:, 0], cot_ref[:, 1], cot_right[...]]
    cots = jnp.concatenate([cot_rows(x) for x in cots], axis=1).astype(bf16)
    wide = dot(cots, spread2[...])
    delta2 = (slope2 * jnp.concatenate([wide, wide], axis=0)).astype(bf16).astype(f32)
    row = lax.broadcasted_iota(jnp.int32, (128, 384), 1) >> 6
    own2 = jnp.where((row >= 1) & (row <= 4), delta2, 0.0).astype(bf16)

    odd = [delta2[:, 128 * j : 128 * j + 128] for j in range(3)]
    odd_taps = [z_taps(x, 64) for x in odd]
    even_taps = [z_taps(between(odd[j], odd[j + 1]), 64) for j in range(2)]
    cols3 = jnp.concatenate(
        [jnp.concatenate([odd_taps[j], even_taps[j], odd_taps[j + 1]], axis=0) for j in range(2)], axis=1
    )
    back = dot(wb_wide, cols3).astype(bf16)
    wide = dot(jnp.concatenate([back[:, :128], back[:, 128:]], axis=0), spread1[...])
    rows = [wide[64 * (i // 2) : 64 * (i // 2) + 64, 128 * (i % 2) : 128 * (i % 2) + 128] for i in range(4)]
    wide = jnp.concatenate([rows[i // 2] for i in range(8)], axis=1)
    delta1 = (slope1 * jnp.concatenate([wide, wide], axis=0)).astype(bf16)

    grad2 = dot_lanes(cols2, own2)
    blocks = []
    for k in range(27):
        p, q, r = k // 9, k // 3 % 3, k % 3
        at = 64 * (3 * p + r)
        blocks.append(
            sum(jnp.where(deep_y == y + 1 - q, grad2[at + 16 * y : at + 16 * y + 16], 0.0) for y in range(4))
        )
    blocks.append(jnp.zeros((16, 128), f32))
    groups = [jnp.concatenate(blocks[7 * j : 7 * j + 7], axis=0) for j in range(4)]
    pay[0:112] = dot_wide(jnp.concatenate(groups, axis=1), gather2[...])

    grad1 = dot_lanes(cols1, delta1).reshape(36, 8, 128)
    groups = [jnp.sum(grad1 * taps_y[q][None], axis=1) for q in range(3)]
    groups = jnp.concatenate([jnp.concatenate(groups, axis=1), jnp.zeros((4, 384), f32)], axis=0)
    pay[112:152] = dot_wide(groups, gather1[...])
    if n_a * part > 152:
        pay[152:] = jnp.zeros((n_a * part - 152, 128), f32)

    def rows_of(t):
        return pl.ds(pl.multiple_of(t * part, 8), part)

    copies = []
    for step in range(1, n_a):
        t, to = in_a(step)
        i = step - 1
        copies.append(remote(pay.at[rows_of(t)], got.at[i], rs_send.at[i], rs_recv.at[i], to))
        copies[-1].start()
    feat_ref[...] = dot_wide(act2[:64] + act2[64:], pool2[...]).astype(bf16).astype(f32)
    total = pay[rows_of(a)]
    for i, copy in enumerate(copies):
        copy.wait_recv()
        total += got[i]

    across[b] = total
    others = []
    for step in range(1, n_b):
        i, to = step - 1, in_b(step)[1]
        others.append(remote(across.at[b], across.at[b], ex_send.at[i], ex_recv.at[i], to))
        others[-1].start()
    for copy in copies:
        copy.wait_send()
    for copy in others:
        copy.wait()
    total = across[0]
    for i in range(1, n_b):
        total += across[i]

    full[rows_of(a)] = total * (1.0 / n_dp)
    copies = []
    for step in range(1, n_a):
        i, to = step - 1, in_a(step)[1]
        copies.append(remote(full.at[rows_of(a)], full.at[rows_of(a)], ag_send.at[i], ag_recv.at[i], to))
        copies[-1].start()
    for copy in copies:
        copy.wait()
    sums_ref[...] = full[0:152]


def unpack(feat_ref, sums_ref, feat_hbm, g1_hbm, g2_hbm, feat_out, g1_out, g2_out, sems):
    for j in range(4):
        many = 7 if j < 3 else 6
        g2_out[7 * j : 7 * j + many] = sums_ref[0 : 16 * many, 32 * j : 32 * j + 32].reshape(many, 16, 32)
    copies = [pltpu.make_async_copy(g2_out, g2_hbm, sems.at[0])]
    copies[0].start()
    for i in range(2):
        feat_out[:, i] = feat_ref[:, 32 * i : 32 * i + 32].reshape(32, 2, 32).astype(bf16)
    copies.append(pltpu.make_async_copy(feat_out, feat_hbm, sems.at[1]))
    copies[1].start()
    for k in range(27):
        p, q, r = k // 9, k // 3 % 3, k % 3
        at = 112 + 4 * (3 * p + r)
        g1_out[k] = sums_ref[at : at + 4, 16 * q : 16 * q + 16]
    copies.append(pltpu.make_async_copy(g1_out, g1_hbm, sems.at[2]))
    copies[2].start()
    for copy in copies:
        copy.wait()


def shards(n_space, n_dp, volumes, first_kernel, middle_kernel, cotangent):
    n_a, n_b = 2 * n_space, n_dp // 2
    part = 8 * -(-152 // (8 * n_a))
    w1 = first_kernel.transpose(2, 3, 4, 1, 0).reshape(27, 4, 16)
    w2 = middle_kernel.transpose(2, 3, 4, 1, 0).reshape(27, 16, 32)
    cot = cotangent[0]
    vol = volumes[0]
    halo = (vol.shape[0], reach) + vol.shape[2:]
    edge = (cot.shape[0],) + cot.shape[2:]
    vmem = pl.BlockSpec(memory_space=pltpu.VMEM)
    hbm = pl.BlockSpec(memory_space=pltpu.HBM)
    dma = pltpu.SemaphoreType.DMA
    feat, sums = pl.pallas_call(
        functools.partial(kernel, n_space, n_dp, part),
        out_shape=(jax.ShapeDtypeStruct((64, 64), f32), jax.ShapeDtypeStruct((152, 128), f32)),
        in_specs=[hbm] * 4,
        out_specs=(vmem, vmem),
        scratch_shapes=[
            pltpu.VMEM(vol.shape, bf16),
            pltpu.VMEM(w1.shape, bf16),
            pltpu.VMEM(w2.shape, bf16),
            pltpu.VMEM(cot.shape, bf16),
            pltpu.VMEM(halo, bf16),
            pltpu.VMEM(halo, bf16),
            pltpu.VMEM(edge, bf16),
            pltpu.VMEM(edge, bf16),
            pltpu.VMEM((n_a * part, 128), f32),
            pltpu.VMEM((n_a - 1, part, 128), f32),
            pltpu.VMEM((n_b, part, 128), f32),
            pltpu.VMEM((n_a * part, 128), f32),
            pltpu.VMEM((256, 128), bf16),
            pltpu.VMEM((384, 64), bf16),
            pltpu.VMEM((128, 256), bf16),
            pltpu.VMEM((128, 384), bf16),
            pltpu.VMEM((384, 128), bf16),
            pltpu.VMEM((512, 128), bf16),
            dma((4,)),
            dma((4,)), dma((4,)),
            dma((n_a - 1,)), dma((n_a - 1,)),
            dma((max(n_b - 1, 1),)), dma((max(n_b - 1, 1),)),
            dma((n_a - 1,)), dma((n_a - 1,)),
        ],
        compiler_params=pltpu.CompilerParams(
            collective_id=0, has_side_effects=True, vmem_limit_bytes=48 * 1024 * 1024
        ),
        cost_estimate=pl.CostEstimate(flops=400_000_000, bytes_accessed=400_000, transcendentals=1_000_000),
    )(*[pltpu.with_memory_space_constraint(x, pltpu.HBM) for x in (vol, w1, w2, cot)])
    features, first_grad, middle_grad = pl.pallas_call(
        unpack,
        out_shape=(
            jax.ShapeDtypeStruct(cot.shape, bf16),
            jax.ShapeDtypeStruct((27, 4, 16), f32),
            jax.ShapeDtypeStruct((27, 16, 32), f32),
        ),
        in_specs=[vmem] * 2,
        out_specs=(hbm, hbm, hbm),
        scratch_shapes=[
            pltpu.VMEM(cot.shape, bf16),
            pltpu.VMEM((27, 4, 16), f32),
            pltpu.VMEM((27, 16, 32), f32),
            dma((3,)),
        ],
    )(feat, sums)
    first_grad = first_grad.reshape(3, 3, 3, 4, 16).transpose(4, 3, 0, 1, 2)
    middle_grad = middle_grad.reshape(3, 3, 3, 16, 32).transpose(4, 3, 0, 1, 2)
    return (features[None], first_grad, middle_grad)


def solution(mesh):
    in_specs = (P("dp", None, "space", None, None), P(), P(), P("dp", None, "space", None, None))
    out_specs = (P("dp", None, "space", None, None), P(), P())
    body = functools.partial(shards, mesh.shape["space"], mesh.shape["dp"])
    return jax.shard_map(body, mesh=mesh, in_specs=in_specs, out_specs=out_specs, check_vma=False)
```

```python
import functools
import math

import jax
import jax.numpy as jnp
from jax import lax
from jax.experimental import pallas as pl
from jax.experimental.pallas import tpu as pltpu
from jax.sharding import PartitionSpec as P

leak_slope = 0.3
soft_share = 0.7
log_two = math.log(2.0)
reach = 5
f32, bf16 = jnp.float32, jnp.bfloat16


def activate(a):
    soft = jnp.maximum(a, 0.0) + jnp.log(1.0 + jnp.exp(-jnp.abs(a)))
    return leak_slope * a + soft_share * (soft - log_two)


def activate_both(a):
    small = jnp.exp(-jnp.abs(a))
    whole = 1.0 + small
    soft = jnp.maximum(a, 0.0) + jnp.log(whole)
    act = leak_slope * a + soft_share * (soft - log_two)
    return act, leak_slope + soft_share * (jnp.where(a >= 0.0, 1.0, small) / whole)


def dot(a, b):
    return jnp.dot(a, b, preferred_element_type=f32)


def dot_lanes(a, b):
    return lax.dot_general(a, b, (((1,), (1,)), ((), ())), preferred_element_type=f32)


def dot_wide(a, b):
    high = a.astype(bf16)
    low = (a - high.astype(f32)).astype(bf16)
    return dot(high, b) + dot(low, b)


def grid_of(rows, cols):
    return (
        lax.broadcasted_iota(jnp.int32, (rows, cols), 0),
        lax.broadcasted_iota(jnp.int32, (rows, cols), 1),
    )


def pick(where, value=1.0):
    return jnp.where(where, value, 0.0).astype(bf16)


def z_taps(a, width):
    place = lax.broadcasted_iota(jnp.int32, a.shape, 1) & (width - 1)
    before = jnp.where(place == 0, 0.0, pltpu.roll(a, 1, 1))
    after = jnp.where(place == width - 1, 0.0, pltpu.roll(a, 127, 1))
    return jnp.concatenate([before, a, after], axis=0).astype(bf16)


def between(a, b):
    place = lax.broadcasted_iota(jnp.int32, a.shape, 1)
    return jnp.where(place < 64, pltpu.roll(a, 64, 1), pltpu.roll(b, 64, 1))


def remote(src, dst, send, recv, to):
    return pltpu.make_async_remote_copy(
        src_ref=src, dst_ref=dst, send_sem=send, recv_sem=recv, device_id=to, device_id_type=pl.DeviceIdType.MESH
    )


def kernel(
    n_space, n_dp, part,
    vol_hbm, w1_hbm, w2_hbm, cot_hbm,
    out_ref,
    vol_ref, w1_ref, w2_ref, cot_ref, vol_left, vol_right, cot_left, cot_right, pay, got, across, full,
    pool1, pool2, spread1, spread2, gather1, gather2,
    load, halo_send, halo_recv, rs_send, rs_recv, ex_send, ex_recv, ag_send, ag_recv,
):
    s, d = lax.axis_index("space"), lax.axis_index("dp")
    n_a, n_b = 2 * n_space, n_dp // 2
    a, b = 2 * s + lax.rem(d, 2), d // 2
    inner = s > 0
    outer = s < n_space - 1

    def in_a(step):
        t = lax.rem(a + step, n_a)
        return t, {"space": t // 2, "dp": 2 * b + lax.rem(t, 2)}

    def in_b(step):
        t = lax.rem(b + step, n_b)
        return t, {"space": s, "dp": 2 * t + lax.rem(d, 2)}

    loads = [
        pltpu.make_async_copy(src, dst, load.at[i])
        for i, (src, dst) in enumerate(
            [(w2_hbm, w2_ref), (w1_hbm, w1_ref), (vol_hbm, vol_ref), (cot_hbm, cot_ref)]
        )
    ]
    for copy in loads:
        copy.start()
    for ref in (vol_left, vol_right, cot_left, cot_right):
        ref[...] = jnp.zeros_like(ref)
    barrier = pltpu.get_barrier_semaphore()
    for step in range(1, n_a):
        pl.semaphore_signal(barrier, inc=1, device_id=in_a(step)[1], device_id_type=pl.DeviceIdType.MESH)
    for step in range(1, n_b):
        pl.semaphore_signal(barrier, inc=1, device_id=in_b(step)[1], device_id_type=pl.DeviceIdType.MESH)
    pl.semaphore_wait(barrier, n_a - 1 + n_b - 1)

    right = {"space": jnp.minimum(s + 1, n_space - 1), "dp": d}
    left = {"space": jnp.maximum(s - 1, 0), "dp": d}
    size_x = vol_hbm.shape[1]
    deep_x = cot_hbm.shape[1]

    def halo(src, dst, sem, to):
        return remote(src, dst, halo_send.at[sem], halo_recv.at[sem], to)

    to_right = [
        halo(vol_hbm.at[:, size_x - reach : size_x], vol_left, 0, right),
        halo(cot_hbm.at[:, deep_x - 1], cot_left, 1, right),
    ]
    to_left = [halo(vol_hbm.at[:, 0:reach], vol_right, 2, left), halo(cot_hbm.at[:, 0], cot_right, 3, left)]

    @pl.when(outer)
    def _():
        for copy in to_right:
            copy.start()

    @pl.when(inner)
    def _():
        for copy in to_left:
            copy.start()

    lane = lax.broadcasted_iota(jnp.int32, (1, 128), 1)
    deep_y = 2 * (lane & 1) + (lane >> 6)
    ro, co = grid_of(32, 128)
    loads[0].wait()
    t2 = dot(w2_ref[...].reshape(27 * 16, 32), pick(ro == (co & 63) >> 1))
    ro, co = grid_of(16, 128)
    loads[1].wait()
    w1 = jnp.concatenate([w1_ref[k].astype(f32) for k in range(27)], axis=0).astype(bf16)
    t1 = dot(w1, pick(ro == (co & 15)))
    ro, co = grid_of(8, 128)
    near_y = 2 * ((co & 63) >> 4) + (co >> 6)
    taps_y = [jnp.where(ro == near_y + q - 1, 1.0, 0.0) for q in range(3)]

    def tap2(k):
        return t2[16 * k : 16 * k + 16]

    w1_rows, w2_rows, wb_cols = [], [], []
    for p in range(3):
        for r in range(3):
            for c in range(4):
                rows = [4 * (9 * p + 3 * q + r) + c for q in range(3)]
                w1_rows.append(sum(t1[k : k + 1] * taps_y[q] for q, k in enumerate(rows)))
            ks = [9 * p + 3 * q + r for q in range(3)]
            block = []
            for y in range(4):
                w2_rows.append(sum(jnp.where(deep_y == y + 1 - q, tap2(k), 0.0) for q, k in enumerate(ks)))
                block.append(sum(jnp.where(deep_y == y + q - 1, tap2(26 - k), 0.0) for q, k in enumerate(ks)))
            wb_cols.append(jnp.concatenate(block, axis=0))
    w1_wide = jnp.concatenate(w1_rows, axis=0).T.astype(bf16)
    w2_wide = jnp.concatenate(w2_rows, axis=0).T.astype(bf16)
    wb_wide = jnp.concatenate(wb_cols, axis=1).astype(bf16)

    def taps_of(ref, i):
        return z_taps(ref[:, i].astype(f32).reshape(32, 128), 128)

    def first_cols(taps):
        count = len(taps) - 2
        return jnp.concatenate([jnp.concatenate(taps[p : p + count], axis=1) for p in range(3)], axis=0)

    loads[2].wait()
    taps_own = [taps_of(vol_ref, i) for i in range(size_x)]
    cols_mid = first_cols(taps_own)
    act_mid, slope_mid = activate_both(dot(w1_wide, cols_mid))
    act_mid = act_mid[:64] + act_mid[64:]

    ro, co = grid_of(256, 128)
    pool1[...] = pick((ro >> 7 == co >> 6) & ((ro & 127) >> 1 == (co & 63)), 0.125)
    ro, co = grid_of(384, 64)
    row = ro >> 6
    same = (row >= 1) & (row <= 4) & ((row - 1) >> 1 == co >> 5) & ((ro & 63) >> 1 == (co & 31))
    pool2[...] = pick(same, 0.125)
    ro, co = grid_of(128, 384)
    spread2[...] = pick((((co >> 6) + 1) >> 1 == ro >> 5) & ((co & 63) >> 1 == (ro & 31)), 0.125)
    ro, co = grid_of(128, 256)
    spread1[...] = pick((ro >> 6 == co >> 7) & ((ro & 63) == (co & 127) >> 1), 0.125)
    ro, co = grid_of(512, 128)
    gather2[...] = pick((ro >> 7 == co >> 5) & ((ro & 63) >> 1 == (co & 31)))
    ro, co = grid_of(896, 128)
    gather1[...] = pick((ro >> 7 == co >> 4) & ((ro & 15) == (co & 15)))

    loads[3].wait()

    @pl.when(outer)
    def _():
        for copy in to_right:
            copy.wait_send()
        for copy in to_left:
            copy.wait_recv()

    @pl.when(inner)
    def _():
        for copy in to_left:
            copy.wait_send()
        for copy in to_right:
            copy.wait_recv()

    taps_low = [taps_of(vol_left, i) for i in range(reach)] + taps_own[:2]
    taps_high = taps_own[-2:] + [taps_of(vol_right, i) for i in range(reach)]
    cols_low, cols_high = first_cols(taps_low), first_cols(taps_high)
    edge = 128 * (reach - 1)
    pre_low, pre_high = dot(w1_wide, cols_low), dot(w1_wide, cols_high)
    act_low, act_high = activate(pre_low[:, :edge]), activate(pre_high[:, 128:])
    act_first, slope_first = activate_both(pre_low[:, edge:])
    act_last, slope_last = activate_both(pre_high[:, :128])
    act1 = [act_low, act_first, None, act_last, act_high]
    act1 = [act_mid if x is None else x[:64] + x[64:] for x in act1]
    act1 = jnp.concatenate(act1, axis=1)
    slope1 = jnp.concatenate([slope_first, slope_mid, slope_last], axis=1)
    cols1 = jnp.concatenate([cols_low[:, edge:], cols_mid, cols_high[:, :128]], axis=1)
    pairs = []
    for j in range(4):
        four = [act1[:, 128 * (4 * j + i) : 128 * (4 * j + i + 1)] for i in range(4)]
        pairs.append(jnp.concatenate([four[0] + four[1], four[2] + four[3]], axis=1))
    acts = dot_wide(jnp.concatenate(pairs, axis=0), pool1[...]).astype(bf16).astype(f32)
    even = [acts[64 * j : 64 * j + 64] for j in range(4)]
    even[0] = jnp.where(inner, even[0], 0.0)
    even[3] = jnp.where(outer, even[3], 0.0)
    odd = [between(even[j], even[j + 1]) for j in range(3)]

    even_taps = [z_taps(x, 64) for x in even]
    odd_taps = [z_taps(x, 64) for x in odd]
    cols2 = jnp.concatenate(
        [jnp.concatenate([even_taps[j], odd_taps[j], even_taps[j + 1]], axis=0) for j in range(3)], axis=1
    )
    act2, slope2 = activate_both(dot(w2_wide, cols2))

    def cot_rows(values):
        return values.astype(f32).reshape(64, 32)

    cots = [cot_left[...], cot_ref[:, 0], cot_ref[:, 1], cot_right[...]]
    cots = jnp.concatenate([cot_rows(x) for x in cots], axis=1).astype(bf16)
    wide = dot(cots, spread2[...])
    delta2 = (slope2 * jnp.concatenate([wide, wide], axis=0)).astype(bf16).astype(f32)
    row = lax.broadcasted_iota(jnp.int32, (128, 384), 1) >> 6
    own2 = jnp.where((row >= 1) & (row <= 4), delta2, 0.0).astype(bf16)

    odd = [delta2[:, 128 * j : 128 * j + 128] for j in range(3)]
    odd_taps = [z_taps(x, 64) for x in odd]
    even_taps = [z_taps(between(odd[j], odd[j + 1]), 64) for j in range(2)]
    cols3 = jnp.concatenate(
        [jnp.concatenate([odd_taps[j], even_taps[j], odd_taps[j + 1]], axis=0) for j in range(2)], axis=1
    )
    back = dot(wb_wide, cols3).astype(bf16)
    wide = dot(jnp.concatenate([back[:, :128], back[:, 128:]], axis=0), spread1[...])
    rows = [wide[64 * (i // 2) : 64 * (i // 2) + 64, 128 * (i % 2) : 128 * (i % 2) + 128] for i in range(4)]
    wide = jnp.concatenate([rows[i // 2] for i in range(8)], axis=1)
    delta1 = (slope1 * jnp.concatenate([wide, wide], axis=0)).astype(bf16)

    grad2 = dot_lanes(cols2, own2)
    blocks = []
    for k in range(27):
        p, q, r = k // 9, k // 3 % 3, k % 3
        at = 64 * (3 * p + r)
        blocks.append(
            sum(jnp.where(deep_y == y + 1 - q, grad2[at + 16 * y : at + 16 * y + 16], 0.0) for y in range(4))
        )
    blocks.append(jnp.zeros((16, 128), f32))
    groups = [jnp.concatenate(blocks[7 * j : 7 * j + 7], axis=0) for j in range(4)]
    pay[0:112] = dot(jnp.concatenate(groups, axis=1).astype(bf16), gather2[...]).astype(bf16)

    grad1 = dot_lanes(cols1, delta1).reshape(36, 8, 128)
    rows = [jnp.sum(grad1 * taps_y[q][None], axis=1) for q in range(3)]
    rows = jnp.concatenate(rows + [jnp.zeros((4, 128), f32)], axis=0)
    groups = jnp.concatenate([rows[16 * j : 16 * j + 16] for j in range(7)], axis=1)
    pay[112:128] = dot(groups.astype(bf16), gather1[...]).astype(bf16)
    if n_a * part > 128:
        pay[128:] = jnp.zeros((n_a * part - 128, 128), bf16)

    def rows_of(t):
        return pl.ds(pl.multiple_of(t * part, 16), part)

    copies = []
    for step in range(1, n_a):
        t, to = in_a(step)
        i = step - 1
        copies.append(remote(pay.at[rows_of(t)], got.at[i], rs_send.at[i], rs_recv.at[i], to))
        copies[-1].start()
    out_ref[128:192, 0:64] = dot_wide(act2[:64] + act2[64:], pool2[...]).astype(bf16).astype(f32)
    total = pay[rows_of(a)].astype(f32)
    for i, copy in enumerate(copies):
        copy.wait_recv()
        total += got[i].astype(f32)

    across[b] = total.astype(bf16)
    others = []
    for step in range(1, n_b):
        i, to = step - 1, in_b(step)[1]
        others.append(remote(across.at[b], across.at[b], ex_send.at[i], ex_recv.at[i], to))
        others[-1].start()
    for copy in copies:
        copy.wait_send()
    for copy in others:
        copy.wait()
    total = across[0].astype(f32)
    for i in range(1, n_b):
        total += across[i].astype(f32)

    full[rows_of(a)] = (total * (1.0 / n_dp)).astype(bf16)
    copies = []
    for step in range(1, n_a):
        i, to = step - 1, in_a(step)[1]
        copies.append(remote(full.at[rows_of(a)], full.at[rows_of(a)], ag_send.at[i], ag_recv.at[i], to))
        copies[-1].start()
    for copy in copies:
        copy.wait()
    out_ref[0:128] = full[0:128].astype(f32)


def unpack(in_ref, feat_hbm, g1_hbm, g2_hbm, feat_out, g1_out, g2_out, sems):
    for j in range(4):
        many = 7 if j < 3 else 6
        g2_out[7 * j : 7 * j + many] = in_ref[0 : 16 * many, 32 * j : 32 * j + 32].reshape(many, 16, 32)
    copies = [pltpu.make_async_copy(g2_out, g2_hbm, sems.at[0])]
    copies[0].start()
    for i in range(2):
        feat_out[:, i] = in_ref[128:192, 32 * i : 32 * i + 32].reshape(32, 2, 32).astype(bf16)
    copies.append(pltpu.make_async_copy(feat_out, feat_hbm, sems.at[1]))
    copies[1].start()
    for k in range(27):
        p, q, r = k // 9, k // 3 % 3, k % 3
        at = 36 * q + 4 * (3 * p + r)
        row, col = 112 + at % 16, 16 * (at // 16)
        g1_out[k] = in_ref[row : row + 4, col : col + 16]
    copies.append(pltpu.make_async_copy(g1_out, g1_hbm, sems.at[2]))
    copies[2].start()
    for copy in copies:
        copy.wait()


def shards(n_space, n_dp, volumes, first_kernel, middle_kernel, cotangent):
    n_a, n_b = 2 * n_space, n_dp // 2
    part = 16 * -(-128 // (16 * n_a))
    w1 = first_kernel.transpose(2, 3, 4, 1, 0).reshape(27, 4, 16)
    w2 = middle_kernel.transpose(2, 3, 4, 1, 0).reshape(27, 16, 32)
    cot = cotangent[0]
    vol = volumes[0]
    halo = (vol.shape[0], reach) + vol.shape[2:]
    edge = (cot.shape[0],) + cot.shape[2:]
    vmem = pl.BlockSpec(memory_space=pltpu.VMEM)
    hbm = pl.BlockSpec(memory_space=pltpu.HBM)
    dma = pltpu.SemaphoreType.DMA
    packed = pl.pallas_call(
        functools.partial(kernel, n_space, n_dp, part),
        out_shape=jax.ShapeDtypeStruct((192, 128), f32),
        in_specs=[hbm] * 4,
        out_specs=vmem,
        scratch_shapes=[
            pltpu.VMEM(vol.shape, bf16),
            pltpu.VMEM(w1.shape, bf16),
            pltpu.VMEM(w2.shape, bf16),
            pltpu.VMEM(cot.shape, bf16),
            pltpu.VMEM(halo, bf16),
            pltpu.VMEM(halo, bf16),
            pltpu.VMEM(edge, bf16),
            pltpu.VMEM(edge, bf16),
            pltpu.VMEM((n_a * part, 128), bf16),
            pltpu.VMEM((n_a - 1, part, 128), bf16),
            pltpu.VMEM((n_b, part, 128), bf16),
            pltpu.VMEM((n_a * part, 128), bf16),
            pltpu.VMEM((256, 128), bf16),
            pltpu.VMEM((384, 64), bf16),
            pltpu.VMEM((128, 256), bf16),
            pltpu.VMEM((128, 384), bf16),
            pltpu.VMEM((896, 128), bf16),
            pltpu.VMEM((512, 128), bf16),
            dma((4,)),
            dma((4,)), dma((4,)),
            dma((n_a - 1,)), dma((n_a - 1,)),
            dma((max(n_b - 1, 1),)), dma((max(n_b - 1, 1),)),
            dma((n_a - 1,)), dma((n_a - 1,)),
        ],
        compiler_params=pltpu.CompilerParams(
            collective_id=0, has_side_effects=True, vmem_limit_bytes=24 * 1024 * 1024
        ),
        cost_estimate=pl.CostEstimate(flops=400_000_000, bytes_accessed=400_000, transcendentals=1_000_000),
    )(*[pltpu.with_memory_space_constraint(x, pltpu.HBM) for x in (vol, w1, w2, cot)])
    features, first_grad, middle_grad = pl.pallas_call(
        unpack,
        out_shape=(
            jax.ShapeDtypeStruct(cot.shape, bf16),
            jax.ShapeDtypeStruct((27, 4, 16), f32),
            jax.ShapeDtypeStruct((27, 16, 32), f32),
        ),
        in_specs=[vmem],
        out_specs=(hbm, hbm, hbm),
        scratch_shapes=[
            pltpu.VMEM(cot.shape, bf16),
            pltpu.VMEM((27, 4, 16), f32),
            pltpu.VMEM((27, 16, 32), f32),
            dma((3,)),
        ],
        compiler_params=pltpu.CompilerParams(vmem_limit_bytes=4 * 1024 * 1024),
    )(packed)
    first_grad = first_grad.reshape(3, 3, 3, 4, 16).transpose(4, 3, 0, 1, 2)
    middle_grad = middle_grad.reshape(3, 3, 3, 16, 32).transpose(4, 3, 0, 1, 2)
    return (features[None], first_grad, middle_grad)


def solution(mesh):
    in_specs = (P("dp", None, "space", None, None), P(), P(), P("dp", None, "space", None, None))
    out_specs = (P("dp", None, "space", None, None), P(), P())
    body = functools.partial(shards, mesh.shape["space"], mesh.shape["dp"])
    return jax.shard_map(body, mesh=mesh, in_specs=in_specs, out_specs=out_specs, check_vma=False)
```

```python
import functools
import math

import jax
import jax.numpy as jnp
from jax import lax
from jax.experimental import pallas as pl
from jax.experimental.pallas import tpu as pltpu
from jax.sharding import PartitionSpec as P

leak_slope = 0.3
soft_share = 0.7
log_two = math.log(2.0)
reach = 5
f32, bf16 = jnp.float32, jnp.bfloat16


def activate(a):
    soft = jnp.maximum(a, 0.0) + jnp.log(1.0 + jnp.exp(-jnp.abs(a)))
    return leak_slope * a + soft_share * (soft - log_two)


def activate_both(a):
    small = jnp.exp(-jnp.abs(a))
    whole = 1.0 + small
    soft = jnp.maximum(a, 0.0) + jnp.log(whole)
    act = leak_slope * a + soft_share * (soft - log_two)
    return act, leak_slope + soft_share * (jnp.where(a >= 0.0, 1.0, small) / whole)


def dot(a, b):
    return jnp.dot(a, b, preferred_element_type=f32)


def dot_lanes(a, b):
    return lax.dot_general(a, b, (((1,), (1,)), ((), ())), preferred_element_type=f32)


def dot_wide(a, b):
    high = a.astype(bf16)
    low = (a - high.astype(f32)).astype(bf16)
    return dot(high, b) + dot(low, b)


def grid_of(rows, cols):
    return (
        lax.broadcasted_iota(jnp.int32, (rows, cols), 0),
        lax.broadcasted_iota(jnp.int32, (rows, cols), 1),
    )


def pick(where, value=1.0):
    return jnp.where(where, value, 0.0).astype(bf16)


def z_taps(a, width):
    place = lax.broadcasted_iota(jnp.int32, a.shape, 1) & (width - 1)
    before = jnp.where(place == 0, 0.0, pltpu.roll(a, 1, 1))
    after = jnp.where(place == width - 1, 0.0, pltpu.roll(a, 127, 1))
    return jnp.concatenate([before, a, after], axis=0).astype(bf16)


def between(a, b):
    place = lax.broadcasted_iota(jnp.int32, a.shape, 1)
    return jnp.where(place < 64, pltpu.roll(a, 64, 1), pltpu.roll(b, 64, 1))


def remote(src, dst, send, recv, to):
    return pltpu.make_async_remote_copy(
        src_ref=src, dst_ref=dst, send_sem=send, recv_sem=recv, device_id=to, device_id_type=pl.DeviceIdType.MESH
    )


def kernel(
    n_space, n_dp, part,
    vol_hbm, w1_hbm, w2_hbm, cot_hbm,
    out_ref,
    vol_ref, w1_ref, w2_ref, cot_ref, vol_left, vol_right, cot_left, cot_right, pay, got, across, full,
    pool1, pool2, spread1, spread2, gather1, gather2,
    load, halo_send, halo_recv, rs_send, rs_recv, ex_send, ex_recv, ag_send, ag_recv,
):
    s, d = lax.axis_index("space"), lax.axis_index("dp")
    n_a, n_b = 2 * n_space, n_dp // 2
    a, b = 2 * s + lax.rem(d, 2), d // 2
    inner = s > 0
    outer = s < n_space - 1

    def in_a(step):
        t = lax.rem(a + step, n_a)
        return t, {"space": t // 2, "dp": 2 * b + lax.rem(t, 2)}

    def in_b(step):
        t = lax.rem(b + step, n_b)
        return t, {"space": s, "dp": 2 * t + lax.rem(d, 2)}

    loads = [
        pltpu.make_async_copy(src, dst, load.at[i])
        for i, (src, dst) in enumerate(
            [(w2_hbm, w2_ref), (w1_hbm, w1_ref), (vol_hbm, vol_ref), (cot_hbm, cot_ref)]
        )
    ]
    for copy in loads:
        copy.start()
    for ref in (vol_left, vol_right, cot_left, cot_right):
        ref[...] = jnp.zeros_like(ref)
    barrier = pltpu.get_barrier_semaphore()
    for step in range(1, n_a):
        pl.semaphore_signal(barrier, inc=1, device_id=in_a(step)[1], device_id_type=pl.DeviceIdType.MESH)
    for step in range(1, n_b):
        pl.semaphore_signal(barrier, inc=1, device_id=in_b(step)[1], device_id_type=pl.DeviceIdType.MESH)
    pl.semaphore_wait(barrier, n_a - 1 + n_b - 1)

    right = {"space": jnp.minimum(s + 1, n_space - 1), "dp": d}
    left = {"space": jnp.maximum(s - 1, 0), "dp": d}
    size_x = vol_hbm.shape[1]
    deep_x = cot_hbm.shape[1]

    def halo(src, dst, sem, to):
        return remote(src, dst, halo_send.at[sem], halo_recv.at[sem], to)

    to_right = [
        halo(vol_hbm.at[:, size_x - reach : size_x], vol_left, 0, right),
        halo(cot_hbm.at[:, deep_x - 1], cot_left, 1, right),
    ]
    to_left = [halo(vol_hbm.at[:, 0:reach], vol_right, 2, left), halo(cot_hbm.at[:, 0], cot_right, 3, left)]

    @pl.when(outer)
    def _():
        for copy in to_right:
            copy.start()

    @pl.when(inner)
    def _():
        for copy in to_left:
            copy.start()

    lane = lax.broadcasted_iota(jnp.int32, (1, 128), 1)
    deep_y = 2 * (lane & 1) + (lane >> 6)
    ro, co = grid_of(32, 128)
    loads[0].wait()
    t2 = dot(w2_ref[...].reshape(27 * 16, 32), pick(ro == (co & 63) >> 1))
    ro, co = grid_of(16, 128)
    loads[1].wait()
    w1 = jnp.concatenate([w1_ref[k].astype(f32) for k in range(27)], axis=0).astype(bf16)
    t1 = dot(w1, pick(ro == (co & 15)))
    ro, co = grid_of(8, 128)
    near_y = 2 * ((co & 63) >> 4) + (co >> 6)
    taps_y = [jnp.where(ro == near_y + q - 1, 1.0, 0.0) for q in range(3)]

    def tap2(k):
        return t2[16 * k : 16 * k + 16]

    w1_rows, w2_rows, wb_cols = [], [], []
    for p in range(3):
        for r in range(3):
            for c in range(4):
                rows = [4 * (9 * p + 3 * q + r) + c for q in range(3)]
                w1_rows.append(sum(t1[k : k + 1] * taps_y[q] for q, k in enumerate(rows)))
            ks = [9 * p + 3 * q + r for q in range(3)]
            block = []
            for y in range(4):
                w2_rows.append(sum(jnp.where(deep_y == y + 1 - q, tap2(k), 0.0) for q, k in enumerate(ks)))
                block.append(sum(jnp.where(deep_y == y + q - 1, tap2(26 - k), 0.0) for q, k in enumerate(ks)))
            wb_cols.append(jnp.concatenate(block, axis=0))
    w1_wide = jnp.concatenate(w1_rows, axis=0).T.astype(bf16)
    w2_wide = jnp.concatenate(w2_rows, axis=0).T.astype(bf16)
    wb_wide = jnp.concatenate(wb_cols, axis=1).astype(bf16)

    def taps_of(ref, i):
        return z_taps(ref[:, i].astype(f32).reshape(32, 128), 128)

    def first_cols(taps):
        count = len(taps) - 2
        return jnp.concatenate([jnp.concatenate(taps[p : p + count], axis=1) for p in range(3)], axis=0)

    loads[2].wait()
    taps_own = [taps_of(vol_ref, i) for i in range(size_x)]
    cols_mid = first_cols(taps_own)
    act_mid, slope_mid = activate_both(dot(w1_wide, cols_mid))
    act_mid = act_mid[:64] + act_mid[64:]

    ro, co = grid_of(256, 128)
    pool1[...] = pick((ro >> 7 == co >> 6) & ((ro & 127) >> 1 == (co & 63)), 0.125)
    ro, co = grid_of(384, 64)
    row = ro >> 6
    same = (row >= 1) & (row <= 4) & ((row - 1) >> 1 == co >> 5) & ((ro & 63) >> 1 == (co & 31))
    pool2[...] = pick(same, 0.125)
    ro, co = grid_of(128, 384)
    spread2[...] = pick((((co >> 6) + 1) >> 1 == ro >> 5) & ((co & 63) >> 1 == (ro & 31)), 0.125)
    ro, co = grid_of(128, 256)
    spread1[...] = pick((ro >> 6 == co >> 7) & ((ro & 63) == (co & 127) >> 1), 0.125)
    ro, co = grid_of(512, 128)
    gather2[...] = pick((ro >> 7 == co >> 5) & ((ro & 63) >> 1 == (co & 31)))
    ro, co = grid_of(896, 128)
    gather1[...] = pick((ro >> 7 == co >> 4) & ((ro & 15) == (co & 15)))

    loads[3].wait()

    @pl.when(outer)
    def _():
        for copy in to_right:
            copy.wait_send()
        for copy in to_left:
            copy.wait_recv()

    @pl.when(inner)
    def _():
        for copy in to_left:
            copy.wait_send()
        for copy in to_right:
            copy.wait_recv()

    taps_low = [taps_of(vol_left, i) for i in range(reach)] + taps_own[:2]
    taps_high = taps_own[-2:] + [taps_of(vol_right, i) for i in range(reach)]
    cols_low, cols_high = first_cols(taps_low), first_cols(taps_high)
    edge = 128 * (reach - 1)
    pre_low, pre_high = dot(w1_wide, cols_low), dot(w1_wide, cols_high)
    act_low, act_high = activate(pre_low[:, :edge]), activate(pre_high[:, 128:])
    act_first, slope_first = activate_both(pre_low[:, edge:])
    act_last, slope_last = activate_both(pre_high[:, :128])
    act1 = [act_low, act_first, None, act_last, act_high]
    act1 = [act_mid if x is None else x[:64] + x[64:] for x in act1]
    act1 = jnp.concatenate(act1, axis=1)
    slope1 = jnp.concatenate([slope_first, slope_mid, slope_last], axis=1)
    cols1 = jnp.concatenate([cols_low[:, edge:], cols_mid, cols_high[:, :128]], axis=1)
    pairs = []
    for j in range(4):
        four = [act1[:, 128 * (4 * j + i) : 128 * (4 * j + i + 1)] for i in range(4)]
        pairs.append(jnp.concatenate([four[0] + four[1], four[2] + four[3]], axis=1))
    acts = dot_wide(jnp.concatenate(pairs, axis=0), pool1[...]).astype(bf16).astype(f32)
    even = [acts[64 * j : 64 * j + 64] for j in range(4)]
    even[0] = jnp.where(inner, even[0], 0.0)
    even[3] = jnp.where(outer, even[3], 0.0)
    odd = [between(even[j], even[j + 1]) for j in range(3)]

    even_taps = [z_taps(x, 64) for x in even]
    odd_taps = [z_taps(x, 64) for x in odd]
    cols2 = jnp.concatenate(
        [jnp.concatenate([even_taps[j], odd_taps[j], even_taps[j + 1]], axis=0) for j in range(3)], axis=1
    )
    act2, slope2 = activate_both(dot(w2_wide, cols2))

    def cot_rows(values):
        return values.astype(f32).reshape(64, 32)

    cots = [cot_left[...], cot_ref[:, 0], cot_ref[:, 1], cot_right[...]]
    cots = jnp.concatenate([cot_rows(x) for x in cots], axis=1).astype(bf16)
    wide = dot(cots, spread2[...])
    delta2 = (slope2 * jnp.concatenate([wide, wide], axis=0)).astype(bf16).astype(f32)
    row = lax.broadcasted_iota(jnp.int32, (128, 384), 1) >> 6
    own2 = jnp.where((row >= 1) & (row <= 4), delta2, 0.0).astype(bf16)

    grad2 = dot_lanes(cols2, own2)
    blocks = []
    for k in range(27):
        p, q, r = k // 9, k // 3 % 3, k % 3
        at = 64 * (3 * p + r)
        blocks.append(
            sum(jnp.where(deep_y == y + 1 - q, grad2[at + 16 * y : at + 16 * y + 16], 0.0) for y in range(4))
        )
    blocks.append(jnp.zeros((16, 128), f32))
    groups = [jnp.concatenate(blocks[7 * j : 7 * j + 7], axis=0) for j in range(4)]
    pay[0:112] = dot(jnp.concatenate(groups, axis=1).astype(bf16), gather2[...]).astype(bf16)
    if n_a * part > 112:
        pay[112:] = jnp.zeros((n_a * part - 112, 128), bf16)

    def rows_of(t):
        return pl.ds(pl.multiple_of(t * part, 16), part)

    parts = []
    for step in range(1, n_a):
        t, to = in_a(step)
        i = step - 1
        parts.append(remote(pay.at[rows_of(t)], got.at[i], rs_send.at[i], rs_recv.at[i], to))
        parts[-1].start()

    odd = [delta2[:, 128 * j : 128 * j + 128] for j in range(3)]
    odd_taps = [z_taps(x, 64) for x in odd]
    even_taps = [z_taps(between(odd[j], odd[j + 1]), 64) for j in range(2)]
    cols3 = jnp.concatenate(
        [jnp.concatenate([odd_taps[j], even_taps[j], odd_taps[j + 1]], axis=0) for j in range(2)], axis=1
    )
    back = dot(wb_wide, cols3).astype(bf16)
    wide = dot(jnp.concatenate([back[:, :128], back[:, 128:]], axis=0), spread1[...])
    rows = [wide[64 * (i // 2) : 64 * (i // 2) + 64, 128 * (i % 2) : 128 * (i % 2) + 128] for i in range(4)]
    wide = jnp.concatenate([rows[i // 2] for i in range(8)], axis=1)
    delta1 = (slope1 * jnp.concatenate([wide, wide], axis=0)).astype(bf16)

    grad1 = dot_lanes(cols1, delta1).reshape(36, 8, 128)
    rows = [jnp.sum(grad1 * taps_y[q][None], axis=1) for q in range(3)]
    rows = jnp.concatenate(rows + [jnp.zeros((4, 128), f32)], axis=0)
    groups = jnp.concatenate([rows[16 * j : 16 * j + 16] for j in range(7)], axis=1)
    across[b, part:] = dot(groups.astype(bf16), gather1[...]).astype(bf16)

    total = pay[rows_of(a)].astype(f32)
    for i, copy in enumerate(parts):
        copy.wait_recv()
        total += got[i].astype(f32)
    across[b, :part] = total.astype(bf16)
    others = []
    for step in range(1, n_b):
        i, to = step - 1, in_b(step)[1]
        others.append(remote(across.at[b], across.at[b], ex_send.at[i], ex_recv.at[i], to))
        others[-1].start()
    out_ref[128:192, 0:64] = dot_wide(act2[:64] + act2[64:], pool2[...]).astype(bf16).astype(f32)
    for copy in parts:
        copy.wait_send()
    for copy in others:
        copy.wait()
    total = across[0].astype(f32)
    for i in range(1, n_b):
        total += across[i].astype(f32)

    full[a] = (total * (1.0 / n_dp)).astype(bf16)
    copies = []
    for step in range(1, n_a):
        i, to = step - 1, in_a(step)[1]
        copies.append(remote(full.at[a], full.at[a], ag_send.at[i], ag_recv.at[i], to))
        copies[-1].start()
    for copy in copies:
        copy.wait()
    for i in range(-(-112 // part)):
        rows = min(part, 112 - part * i)
        out_ref[part * i : part * i + rows] = full[i, :rows].astype(f32)
    total = full[0, part:].astype(f32)
    for i in range(1, n_a):
        total += full[i, part:].astype(f32)
    out_ref[112:128] = total


def unpack(in_ref, feat_hbm, g1_hbm, g2_hbm, feat_out, g1_out, g2_out, sems):
    for j in range(4):
        many = 7 if j < 3 else 6
        g2_out[7 * j : 7 * j + many] = in_ref[0 : 16 * many, 32 * j : 32 * j + 32].reshape(many, 16, 32)
    copies = [pltpu.make_async_copy(g2_out, g2_hbm, sems.at[0])]
    copies[0].start()
    for i in range(2):
        feat_out[:, i] = in_ref[128:192, 32 * i : 32 * i + 32].reshape(32, 2, 32).astype(bf16)
    copies.append(pltpu.make_async_copy(feat_out, feat_hbm, sems.at[1]))
    copies[1].start()
    for k in range(27):
        p, q, r = k // 9, k // 3 % 3, k % 3
        at = 36 * q + 4 * (3 * p + r)
        row, col = 112 + at % 16, 16 * (at // 16)
        g1_out[k] = in_ref[row : row + 4, col : col + 16]
    copies.append(pltpu.make_async_copy(g1_out, g1_hbm, sems.at[2]))
    copies[2].start()
    for copy in copies:
        copy.wait()


def shards(n_space, n_dp, volumes, first_kernel, middle_kernel, cotangent):
    n_a, n_b = 2 * n_space, n_dp // 2
    part = 16 * -(-112 // (16 * n_a))
    w1 = first_kernel.transpose(2, 3, 4, 1, 0).reshape(27, 4, 16)
    w2 = middle_kernel.transpose(2, 3, 4, 1, 0).reshape(27, 16, 32)
    cot = cotangent[0]
    vol = volumes[0]
    halo = (vol.shape[0], reach) + vol.shape[2:]
    edge = (cot.shape[0],) + cot.shape[2:]
    vmem = pl.BlockSpec(memory_space=pltpu.VMEM)
    hbm = pl.BlockSpec(memory_space=pltpu.HBM)
    dma = pltpu.SemaphoreType.DMA
    packed = pl.pallas_call(
        functools.partial(kernel, n_space, n_dp, part),
        out_shape=jax.ShapeDtypeStruct((192, 128), f32),
        in_specs=[hbm] * 4,
        out_specs=vmem,
        scratch_shapes=[
            pltpu.VMEM(vol.shape, bf16),
            pltpu.VMEM(w1.shape, bf16),
            pltpu.VMEM(w2.shape, bf16),
            pltpu.VMEM(cot.shape, bf16),
            pltpu.VMEM(halo, bf16),
            pltpu.VMEM(halo, bf16),
            pltpu.VMEM(edge, bf16),
            pltpu.VMEM(edge, bf16),
            pltpu.VMEM((n_a * part, 128), bf16),
            pltpu.VMEM((n_a - 1, part, 128), bf16),
            pltpu.VMEM((n_b, part + 16, 128), bf16),
            pltpu.VMEM((n_a, part + 16, 128), bf16),
            pltpu.VMEM((256, 128), bf16),
            pltpu.VMEM((384, 64), bf16),
            pltpu.VMEM((128, 256), bf16),
            pltpu.VMEM((128, 384), bf16),
            pltpu.VMEM((896, 128), bf16),
            pltpu.VMEM((512, 128), bf16),
            dma((4,)),
            dma((4,)), dma((4,)),
            dma((n_a - 1,)), dma((n_a - 1,)),
            dma((max(n_b - 1, 1),)), dma((max(n_b - 1, 1),)),
            dma((n_a - 1,)), dma((n_a - 1,)),
        ],
        compiler_params=pltpu.CompilerParams(
            collective_id=0, has_side_effects=True, vmem_limit_bytes=24 * 1024 * 1024
        ),
        cost_estimate=pl.CostEstimate(flops=400_000_000, bytes_accessed=400_000, transcendentals=1_000_000),
    )(*[pltpu.with_memory_space_constraint(x, pltpu.HBM) for x in (vol, w1, w2, cot)])
    features, first_grad, middle_grad = pl.pallas_call(
        unpack,
        out_shape=(
            jax.ShapeDtypeStruct(cot.shape, bf16),
            jax.ShapeDtypeStruct((27, 4, 16), f32),
            jax.ShapeDtypeStruct((27, 16, 32), f32),
        ),
        in_specs=[vmem],
        out_specs=(hbm, hbm, hbm),
        scratch_shapes=[
            pltpu.VMEM(cot.shape, bf16),
            pltpu.VMEM((27, 4, 16), f32),
            pltpu.VMEM((27, 16, 32), f32),
            dma((3,)),
        ],
        compiler_params=pltpu.CompilerParams(vmem_limit_bytes=4 * 1024 * 1024),
    )(packed)
    first_grad = first_grad.reshape(3, 3, 3, 4, 16).transpose(4, 3, 0, 1, 2)
    middle_grad = middle_grad.reshape(3, 3, 3, 16, 32).transpose(4, 3, 0, 1, 2)
    return (features[None], first_grad, middle_grad)


def solution(mesh):
    in_specs = (P("dp", None, "space", None, None), P(), P(), P("dp", None, "space", None, None))
    out_specs = (P("dp", None, "space", None, None), P(), P())
    body = functools.partial(shards, mesh.shape["space"], mesh.shape["dp"])
    return jax.shard_map(body, mesh=mesh, in_specs=in_specs, out_specs=out_specs, check_vma=False)
```

```python
import functools
import math

import jax
import jax.numpy as jnp
import numpy as np
from jax import lax
from jax.experimental import pallas as pl
from jax.experimental.pallas import tpu as pltpu
from jax.sharding import PartitionSpec as P

leak_slope = 0.3
soft_share = 0.7
log_two = math.log(2.0)
reach = 5
f32, bf16 = jnp.float32, jnp.bfloat16


def soft_terms(a):
    return jnp.maximum(leak_slope * a, a), 1.0 + jnp.exp(-jnp.abs(a))


def halves(terms):
    x, y = terms
    return x[:64] + x[64:], y[:64] * y[64:]


def act_sum(x, y, count):
    return x + soft_share * (jnp.log(y) - count * log_two)


def slope_of(a):
    return (leak_slope + 0.5 * soft_share) + 0.5 * soft_share * jnp.tanh(0.5 * a)


def dot(a, b):
    return jnp.dot(a, b, preferred_element_type=f32)


def dot_lanes(a, b):
    return lax.dot_general(a, b, (((1,), (1,)), ((), ())), preferred_element_type=f32)


def grid_of(rows, cols):
    return (
        lax.broadcasted_iota(jnp.int32, (rows, cols), 0),
        lax.broadcasted_iota(jnp.int32, (rows, cols), 1),
    )


def pick(where, value=1.0):
    return jnp.where(where, value, 0.0).astype(bf16)


def tables():
    def table(rows, cols, rule):
        return rule(np.arange(rows)[:, None], np.arange(cols)[None, :])

    pool1 = table(256, 128, lambda r, c: (r >> 7 == c >> 6) & ((r & 127) >> 1 == (c & 63))) * 0.125
    row = (np.arange(384) >> 6)[:, None]
    pool2 = table(384, 128, lambda r, c: ((r & 63) >> 1 == (c & 31)) & (c < 64) & ((row - 1) >> 1 == c >> 5))
    pool2 = pool2 * 0.125 * ((row >= 1) & (row <= 4))
    spread1 = table(128, 256, lambda r, c: (r >> 6 == c >> 7) & ((r & 63) == (c & 127) >> 1)) * 0.125
    spread2 = table(128, 384, lambda r, c: (((c >> 6) + 1) >> 1 == r >> 5) & ((c & 63) >> 1 == (r & 31))) * 0.125
    gather1 = table(896, 128, lambda r, c: (r >> 7 == c >> 4) & ((r & 15) == (c & 15)))
    gather2 = table(512, 128, lambda r, c: (r >> 7 == c >> 5) & ((r & 63) >> 1 == (c & 31)))
    parts = [pool1, pool2, *np.split(spread1, 2, 1), *np.split(spread2, 3, 1), gather1, gather2]
    return np.concatenate(parts, 0).astype(np.float32).astype(bf16)


at_pool1, at_pool2, at_spread1, at_spread2, at_gather1, at_gather2 = 0, 256, 640, 896, 1280, 2176


def z_taps(a, width):
    place = lax.broadcasted_iota(jnp.int32, a.shape, 1) & (width - 1)
    before = jnp.where(place == 0, 0.0, pltpu.roll(a, 1, 1))
    after = jnp.where(place == width - 1, 0.0, pltpu.roll(a, 127, 1))
    return jnp.concatenate([before, a, after], axis=0).astype(bf16)


def between(a, b):
    place = lax.broadcasted_iota(jnp.int32, a.shape, 1)
    return jnp.where(place < 64, pltpu.roll(a, 64, 1), pltpu.roll(b, 64, 1))


def remote(src, dst, send, recv, to):
    return pltpu.make_async_remote_copy(
        src_ref=src, dst_ref=dst, send_sem=send, recv_sem=recv, device_id=to, device_id_type=pl.DeviceIdType.MESH
    )


def kernel(
    n_space, n_dp, part,
    vol_hbm, w1_hbm, w2_hbm, cot_hbm, table_hbm,
    out_ref,
    vol_ref, w1_ref, w2_ref, cot_ref, vol_left, vol_right, cot_left, cot_right, pay, got, across, full,
    table_ref,
    load, halo_send, halo_recv, rs_send, rs_recv, ex_send, ex_recv, ag_send, ag_recv,
):
    s, d = lax.axis_index("space"), lax.axis_index("dp")
    n_a, n_b = 2 * n_space, n_dp // 2
    a, b = 2 * s + lax.rem(d, 2), d // 2
    inner = s > 0
    outer = s < n_space - 1

    def in_a(step):
        t = lax.rem(a + step, n_a)
        return t, {"space": t // 2, "dp": 2 * b + lax.rem(t, 2)}

    def in_b(step):
        t = lax.rem(b + step, n_b)
        return t, {"space": s, "dp": 2 * t + lax.rem(d, 2)}

    loads = [
        pltpu.make_async_copy(src, dst, load.at[i])
        for i, (src, dst) in enumerate(
            [(w2_hbm, w2_ref), (w1_hbm, w1_ref), (vol_hbm, vol_ref), (cot_hbm, cot_ref), (table_hbm, table_ref)]
        )
    ]
    for copy in loads:
        copy.start()
    for ref in (vol_left, vol_right, cot_left, cot_right):
        ref[...] = jnp.zeros_like(ref)
    barrier = pltpu.get_barrier_semaphore()
    for step in range(1, n_a):
        pl.semaphore_signal(barrier, inc=1, device_id=in_a(step)[1], device_id_type=pl.DeviceIdType.MESH)
    for step in range(1, n_b):
        pl.semaphore_signal(barrier, inc=1, device_id=in_b(step)[1], device_id_type=pl.DeviceIdType.MESH)
    pl.semaphore_wait(barrier, n_a - 1 + n_b - 1)

    right = {"space": jnp.minimum(s + 1, n_space - 1), "dp": d}
    left = {"space": jnp.maximum(s - 1, 0), "dp": d}
    size_x = vol_hbm.shape[1]
    deep_x = cot_hbm.shape[1]

    def halo(src, dst, sem, to):
        return remote(src, dst, halo_send.at[sem], halo_recv.at[sem], to)

    to_right = [
        halo(vol_hbm.at[:, size_x - reach : size_x], vol_left, 0, right),
        halo(cot_hbm.at[:, deep_x - 1], cot_left, 1, right),
    ]
    to_left = [halo(vol_hbm.at[:, 0:reach], vol_right, 2, left), halo(cot_hbm.at[:, 0], cot_right, 3, left)]

    @pl.when(outer)
    def _():
        for copy in to_right:
            copy.start()

    @pl.when(inner)
    def _():
        for copy in to_left:
            copy.start()

    lane = lax.broadcasted_iota(jnp.int32, (1, 128), 1)
    deep_y = 2 * (lane & 1) + (lane >> 6)
    ro, co = grid_of(32, 128)
    loads[0].wait()
    t2 = dot(w2_ref[...].reshape(27 * 16, 32), pick(ro == (co & 63) >> 1))
    ro, co = grid_of(16, 128)
    loads[1].wait()
    w1 = jnp.concatenate([w1_ref[k].astype(f32) for k in range(27)], axis=0).astype(bf16)
    t1 = dot(w1, pick(ro == (co & 15)))
    ro, co = grid_of(8, 128)
    near_y = 2 * ((co & 63) >> 4) + (co >> 6)
    taps_y = [jnp.where(ro == near_y + q - 1, 1.0, 0.0) for q in range(3)]

    def tap2(k):
        return t2[16 * k : 16 * k + 16]

    w1_rows, w2_rows, wb_cols = [], [], []
    for p in range(3):
        for r in range(3):
            for c in range(4):
                rows = [4 * (9 * p + 3 * q + r) + c for q in range(3)]
                w1_rows.append(sum(t1[k : k + 1] * taps_y[q] for q, k in enumerate(rows)))
            ks = [9 * p + 3 * q + r for q in range(3)]
            block = []
            for y in range(4):
                w2_rows.append(sum(jnp.where(deep_y == y + 1 - q, tap2(k), 0.0) for q, k in enumerate(ks)))
                block.append(sum(jnp.where(deep_y == y + q - 1, tap2(26 - k), 0.0) for q, k in enumerate(ks)))
            wb_cols.append(jnp.concatenate(block, axis=0))
    w1_wide = jnp.concatenate(w1_rows, axis=0).T.astype(bf16)
    w2_wide = jnp.concatenate(w2_rows, axis=0).T.astype(bf16)
    wb_wide = jnp.concatenate(wb_cols, axis=1).astype(bf16)

    def taps_of(ref, i):
        return z_taps(ref[:, i].astype(f32).reshape(32, 128), 128)

    def first_cols(taps):
        count = len(taps) - 2
        return jnp.concatenate([jnp.concatenate(taps[p : p + count], axis=1) for p in range(3)], axis=0)

    loads[2].wait()
    taps_own = [taps_of(vol_ref, i) for i in range(size_x)]
    cols_mid = first_cols(taps_own)
    pre_mid = dot(w1_wide, cols_mid)
    sums_mid, slope_mid = halves(soft_terms(pre_mid)), slope_of(pre_mid)

    loads[3].wait()
    loads[4].wait()

    @pl.when(outer)
    def _():
        for copy in to_right:
            copy.wait_send()
        for copy in to_left:
            copy.wait_recv()

    @pl.when(inner)
    def _():
        for copy in to_left:
            copy.wait_send()
        for copy in to_right:
            copy.wait_recv()

    taps_low = [taps_of(vol_left, i) for i in range(reach)] + taps_own[:2]
    taps_high = taps_own[-2:] + [taps_of(vol_right, i) for i in range(reach)]
    cols_low, cols_high = first_cols(taps_low), first_cols(taps_high)
    edge = 128 * (reach - 1)
    pre_low, pre_high = dot(w1_wide, cols_low), dot(w1_wide, cols_high)
    sums = [halves(soft_terms(pre_low)), sums_mid, halves(soft_terms(pre_high))]
    sum_x, sum_y = [jnp.concatenate(x, axis=1) for x in zip(*sums)]
    slope1 = jnp.concatenate([slope_of(pre_low[:, edge:]), slope_mid, slope_of(pre_high[:, :128])], axis=1)
    cols1 = jnp.concatenate([cols_low[:, edge:], cols_mid, cols_high[:, :128]], axis=1)
    pairs = []
    for j in range(4):
        pair = []
        for at in (512 * j, 512 * j + 256):
            x = sum_x[:, at : at + 128] + sum_x[:, at + 128 : at + 256]
            y = sum_y[:, at : at + 128] * sum_y[:, at + 128 : at + 256]
            pair.append(act_sum(x, y, 4))
        pairs.append(jnp.concatenate(pair, axis=1))
    pool = table_ref[at_pool1 : at_pool1 + 256]
    acts = dot(jnp.concatenate(pairs, axis=0).astype(bf16), pool).astype(bf16).astype(f32)
    even = [acts[64 * j : 64 * j + 64] for j in range(4)]
    even[0] = jnp.where(inner, even[0], 0.0)
    even[3] = jnp.where(outer, even[3], 0.0)
    odd = [between(even[j], even[j + 1]) for j in range(3)]

    even_taps = [z_taps(x, 64) for x in even]
    odd_taps = [z_taps(x, 64) for x in odd]
    cols2 = jnp.concatenate(
        [jnp.concatenate([even_taps[j], odd_taps[j], even_taps[j + 1]], axis=0) for j in range(3)], axis=1
    )
    pre2 = dot(w2_wide, cols2)
    slope2 = slope_of(pre2)

    def cot_rows(values):
        return values.astype(f32).reshape(64, 32)

    cots = [cot_left[...], cot_ref[:, 0], cot_ref[:, 1], cot_right[...]]
    cots = jnp.concatenate([cot_rows(x) for x in cots], axis=1).astype(bf16)
    wide = [dot(cots, table_ref[at : at + 128]) for at in range(at_spread2, at_spread2 + 384, 128)]
    wide = jnp.concatenate(wide, axis=1)
    delta2 = (slope2 * jnp.concatenate([wide, wide], axis=0)).astype(bf16).astype(f32)
    row = lax.broadcasted_iota(jnp.int32, (128, 384), 1) >> 6
    own2 = jnp.where((row >= 1) & (row <= 4), delta2, 0.0).astype(bf16)

    grad2 = dot_lanes(cols2, own2)
    blocks = []
    for k in range(27):
        p, q, r = k // 9, k // 3 % 3, k % 3
        at = 64 * (3 * p + r)
        blocks.append(
            sum(jnp.where(deep_y == y + 1 - q, grad2[at + 16 * y : at + 16 * y + 16], 0.0) for y in range(4))
        )
    blocks.append(jnp.zeros((16, 128), f32))
    groups = [jnp.concatenate(blocks[7 * j : 7 * j + 7], axis=0) for j in range(4)]
    pay[0:112] = dot(jnp.concatenate(groups, axis=1).astype(bf16), table_ref[at_gather2 : at_gather2 + 512]).astype(bf16)
    if n_a * part > 112:
        pay[112:] = jnp.zeros((n_a * part - 112, 128), bf16)

    def rows_of(t):
        return pl.ds(pl.multiple_of(t * part, 16), part)

    parts = []
    for step in range(1, n_a):
        t, to = in_a(step)
        i = step - 1
        parts.append(remote(pay.at[rows_of(t)], got.at[i], rs_send.at[i], rs_recv.at[i], to))
        parts[-1].start()

    odd = [delta2[:, 128 * j : 128 * j + 128] for j in range(3)]
    odd_taps = [z_taps(x, 64) for x in odd]
    even_taps = [z_taps(between(odd[j], odd[j + 1]), 64) for j in range(2)]
    cols3 = jnp.concatenate(
        [jnp.concatenate([odd_taps[j], even_taps[j], odd_taps[j + 1]], axis=0) for j in range(2)], axis=1
    )
    back = dot(wb_wide, cols3).astype(bf16)
    spread = jnp.concatenate([table_ref[at : at + 128] for at in (at_spread1, at_spread1 + 128)], axis=1)
    wide = dot(jnp.concatenate([back[:, :128], back[:, 128:]], axis=0), spread)
    rows = [wide[64 * (i // 2) : 64 * (i // 2) + 64, 128 * (i % 2) : 128 * (i % 2) + 128] for i in range(4)]
    wide = jnp.concatenate([rows[i // 2] for i in range(8)], axis=1)
    delta1 = (slope1 * jnp.concatenate([wide, wide], axis=0)).astype(bf16)

    grad1 = dot_lanes(cols1, delta1).reshape(36, 8, 128)
    rows = [jnp.sum(grad1 * taps_y[q][None], axis=1) for q in range(3)]
    rows = jnp.concatenate(rows + [jnp.zeros((4, 128), f32)], axis=0)
    groups = jnp.concatenate([rows[16 * j : 16 * j + 16] for j in range(7)], axis=1)
    across[b, part:] = dot(groups.astype(bf16), table_ref[at_gather1 : at_gather1 + 896]).astype(bf16)

    total = pay[rows_of(a)].astype(f32)
    for i, copy in enumerate(parts):
        copy.wait_recv()
        total += got[i].astype(f32)
    across[b, :part] = total.astype(bf16)
    others = []
    for step in range(1, n_b):
        i, to = step - 1, in_b(step)[1]
        others.append(remote(across.at[b], across.at[b], ex_send.at[i], ex_recv.at[i], to))
        others[-1].start()
    act2 = act_sum(*halves(soft_terms(pre2)), 2).astype(bf16)
    out_ref[128:192] = dot(act2, table_ref[at_pool2 : at_pool2 + 384]).astype(bf16).astype(f32)
    for copy in parts:
        copy.wait_send()
    for copy in others:
        copy.wait()
    total = across[0].astype(f32)
    for i in range(1, n_b):
        total += across[i].astype(f32)

    full[a] = (total * (1.0 / n_dp)).astype(bf16)
    copies = []
    for step in range(1, n_a):
        i, to = step - 1, in_a(step)[1]
        copies.append(remote(full.at[a], full.at[a], ag_send.at[i], ag_recv.at[i], to))
        copies[-1].start()
    for copy in copies:
        copy.wait()
    for i in range(-(-112 // part)):
        rows = min(part, 112 - part * i)
        out_ref[part * i : part * i + rows] = full[i, :rows].astype(f32)
    total = full[0, part:].astype(f32)
    for i in range(1, n_a):
        total += full[i, part:].astype(f32)
    out_ref[112:128] = total


def unpack(in_ref, feat_hbm, g1_hbm, g2_hbm, feat_out, g1_out, g2_out, sems):
    for j in range(4):
        many = 7 if j < 3 else 6
        g2_out[7 * j : 7 * j + many] = in_ref[0 : 16 * many, 32 * j : 32 * j + 32].reshape(many, 16, 32)
    copies = [pltpu.make_async_copy(g2_out, g2_hbm, sems.at[0])]
    copies[0].start()
    for i in range(2):
        feat_out[:, i] = in_ref[128:192, 32 * i : 32 * i + 32].reshape(32, 2, 32).astype(bf16)
    copies.append(pltpu.make_async_copy(feat_out, feat_hbm, sems.at[1]))
    copies[1].start()
    for k in range(27):
        p, q, r = k // 9, k // 3 % 3, k % 3
        at = 36 * q + 4 * (3 * p + r)
        row, col = 112 + at % 16, 16 * (at // 16)
        g1_out[k] = in_ref[row : row + 4, col : col + 16]
    copies.append(pltpu.make_async_copy(g1_out, g1_hbm, sems.at[2]))
    copies[2].start()
    for copy in copies:
        copy.wait()


def shards(n_space, n_dp, volumes, first_kernel, middle_kernel, cotangent):
    n_a, n_b = 2 * n_space, n_dp // 2
    part = 16 * -(-112 // (16 * n_a))
    w1 = first_kernel.transpose(2, 3, 4, 1, 0).reshape(27, 4, 16)
    w2 = middle_kernel.transpose(2, 3, 4, 1, 0).reshape(27, 16, 32)
    cot = cotangent[0]
    vol = volumes[0]
    table = jnp.asarray(tables())
    halo = (vol.shape[0], reach) + vol.shape[2:]
    edge = (cot.shape[0],) + cot.shape[2:]
    vmem = pl.BlockSpec(memory_space=pltpu.VMEM)
    hbm = pl.BlockSpec(memory_space=pltpu.HBM)
    dma = pltpu.SemaphoreType.DMA
    packed = pl.pallas_call(
        functools.partial(kernel, n_space, n_dp, part),
        out_shape=jax.ShapeDtypeStruct((192, 128), f32),
        in_specs=[hbm] * 5,
        out_specs=vmem,
        scratch_shapes=[
            pltpu.VMEM(vol.shape, bf16),
            pltpu.VMEM(w1.shape, bf16),
            pltpu.VMEM(w2.shape, bf16),
            pltpu.VMEM(cot.shape, bf16),
            pltpu.VMEM(halo, bf16),
            pltpu.VMEM(halo, bf16),
            pltpu.VMEM(edge, bf16),
            pltpu.VMEM(edge, bf16),
            pltpu.VMEM((n_a * part, 128), bf16),
            pltpu.VMEM((n_a - 1, part, 128), bf16),
            pltpu.VMEM((n_b, part + 16, 128), bf16),
            pltpu.VMEM((n_a, part + 16, 128), bf16),
            pltpu.VMEM(table.shape, bf16),
            dma((5,)),
            dma((4,)), dma((4,)),
            dma((n_a - 1,)), dma((n_a - 1,)),
            dma((max(n_b - 1, 1),)), dma((max(n_b - 1, 1),)),
            dma((n_a - 1,)), dma((n_a - 1,)),
        ],
        compiler_params=pltpu.CompilerParams(
            collective_id=0, has_side_effects=True, vmem_limit_bytes=24 * 1024 * 1024
        ),
        cost_estimate=pl.CostEstimate(flops=400_000_000, bytes_accessed=400_000, transcendentals=1_000_000),
    )(*[pltpu.with_memory_space_constraint(x, pltpu.HBM) for x in (vol, w1, w2, cot, table)])
    features, first_grad, middle_grad = pl.pallas_call(
        unpack,
        out_shape=(
            jax.ShapeDtypeStruct(cot.shape, bf16),
            jax.ShapeDtypeStruct((27, 4, 16), f32),
            jax.ShapeDtypeStruct((27, 16, 32), f32),
        ),
        in_specs=[vmem],
        out_specs=(hbm, hbm, hbm),
        scratch_shapes=[
            pltpu.VMEM(cot.shape, bf16),
            pltpu.VMEM((27, 4, 16), f32),
            pltpu.VMEM((27, 16, 32), f32),
            dma((3,)),
        ],
        compiler_params=pltpu.CompilerParams(vmem_limit_bytes=4 * 1024 * 1024),
    )(packed)
    first_grad = first_grad.reshape(3, 3, 3, 4, 16).transpose(4, 3, 0, 1, 2)
    middle_grad = middle_grad.reshape(3, 3, 3, 16, 32).transpose(4, 3, 0, 1, 2)
    return (features[None], first_grad, middle_grad)


def solution(mesh):
    in_specs = (P("dp", None, "space", None, None), P(), P(), P("dp", None, "space", None, None))
    out_specs = (P("dp", None, "space", None, None), P(), P())
    body = functools.partial(shards, mesh.shape["space"], mesh.shape["dp"])
    return jax.shard_map(body, mesh=mesh, in_specs=in_specs, out_specs=out_specs, check_vma=False)
```

```python
import functools
import math

import jax
import jax.numpy as jnp
import numpy as np
from jax import lax
from jax.experimental import pallas as pl
from jax.experimental.pallas import tpu as pltpu
from jax.sharding import PartitionSpec as P

leak_slope = 0.3
soft_share = 0.7
log_two = math.log(2.0)
reach = 5
f32, bf16 = jnp.float32, jnp.bfloat16


def soft_terms(a):
    return jnp.maximum(leak_slope * a, a), 1.0 + jnp.exp(-jnp.abs(a))


def halves(terms):
    x, y = terms
    return x[:64] + x[64:], y[:64] * y[64:]


def act_sum(x, y, count):
    return x + soft_share * (jnp.log(y) - count * log_two)


def slope_of(a):
    return (leak_slope + 0.5 * soft_share) + 0.5 * soft_share * jnp.tanh(0.5 * a)


def dot(a, b):
    return jnp.dot(a, b, preferred_element_type=f32)


def dot_lanes(a, b):
    return lax.dot_general(a, b, (((1,), (1,)), ((), ())), preferred_element_type=f32)


def grid_of(rows, cols):
    return (
        lax.broadcasted_iota(jnp.int32, (rows, cols), 0),
        lax.broadcasted_iota(jnp.int32, (rows, cols), 1),
    )


def pick(where, value=1.0):
    return jnp.where(where, value, 0.0).astype(bf16)


def tables():
    def table(rows, cols, rule):
        return rule(np.arange(rows)[:, None], np.arange(cols)[None, :])

    pool1 = table(256, 128, lambda r, c: (r >> 7 == c >> 6) & ((r & 127) >> 1 == (c & 63))) * 0.125
    row = (np.arange(384) >> 6)[:, None]
    pool2 = table(384, 128, lambda r, c: ((r & 63) >> 1 == (c & 31)) & (c < 64) & ((row - 1) >> 1 == c >> 5))
    pool2 = pool2 * 0.125 * ((row >= 1) & (row <= 4))
    spread1 = table(128, 256, lambda r, c: (r >> 6 == c >> 7) & ((r & 63) == (c & 127) >> 1)) * 0.125
    spread2 = table(128, 384, lambda r, c: (((c >> 6) + 1) >> 1 == r >> 5) & ((c & 63) >> 1 == (r & 31))) * 0.125
    gather1 = table(896, 128, lambda r, c: (r >> 7 == c >> 4) & ((r & 15) == (c & 15)))
    gather2 = table(512, 128, lambda r, c: (r >> 7 == c >> 5) & ((r & 63) >> 1 == (c & 31)))
    parts = [pool1, pool2, *np.split(spread1, 2, 1), *np.split(spread2, 3, 1), gather1, gather2]
    return np.concatenate(parts, 0).astype(np.float32).astype(bf16)


at_pool1, at_pool2, at_spread1, at_spread2, at_gather1, at_gather2 = 0, 256, 640, 896, 1280, 2176


def z_taps(a, width):
    place = lax.broadcasted_iota(jnp.int32, a.shape, 1) & (width - 1)
    before = jnp.where(place == 0, 0.0, pltpu.roll(a, 1, 1))
    after = jnp.where(place == width - 1, 0.0, pltpu.roll(a, 127, 1))
    return jnp.concatenate([before, a, after], axis=0).astype(bf16)


def between(a, b):
    place = lax.broadcasted_iota(jnp.int32, a.shape, 1)
    return jnp.where(place < 64, pltpu.roll(a, 64, 1), pltpu.roll(b, 64, 1))


def remote(src, dst, send, recv, to):
    return pltpu.make_async_remote_copy(
        src_ref=src, dst_ref=dst, send_sem=send, recv_sem=recv, device_id=to, device_id_type=pl.DeviceIdType.MESH
    )


def kernel(
    n_space, n_dp, part,
    vol_hbm, w1_hbm, w2_hbm, cot_hbm, table_hbm,
    out_ref,
    vol_ref, w1_ref, w2_ref, cot_ref, vol_left, vol_right, cot_left, cot_right, pay, got, across, full,
    table_ref,
    load, halo_send, halo_recv, rs_send, rs_recv, ex_send, ex_recv, ag_send, ag_recv,
):
    s, d = lax.axis_index("space"), lax.axis_index("dp")
    n_a, n_b = 2 * n_space, n_dp // 2
    a, b = 2 * s + lax.rem(d, 2), d // 2
    inner = s > 0
    outer = s < n_space - 1
    size_x, deep_x = vol_hbm.shape[1], cot_hbm.shape[1]

    def in_a(step):
        t = lax.rem(a + step, n_a)
        return t, {"space": t // 2, "dp": 2 * b + lax.rem(t, 2)}

    def in_b(step):
        t = lax.rem(b + step, n_b)
        return t, {"space": s, "dp": 2 * t + lax.rem(d, 2)}

    loads = [
        pltpu.make_async_copy(src, dst, load.at[i])
        for i, (src, dst) in enumerate(
            [(w2_hbm, w2_ref), (w1_hbm, w1_ref), (vol_hbm, vol_ref), (cot_hbm, cot_ref), (table_hbm, table_ref)]
        )
    ]
    for copy in loads:
        copy.start()
    for ref in (vol_left, vol_right, cot_left, cot_right):
        ref[...] = jnp.zeros_like(ref)
    barrier = pltpu.get_barrier_semaphore()
    for step in range(1, n_a):
        pl.semaphore_signal(barrier, inc=1, device_id=in_a(step)[1], device_id_type=pl.DeviceIdType.MESH)
    for step in range(1, n_b):
        pl.semaphore_signal(barrier, inc=1, device_id=in_b(step)[1], device_id_type=pl.DeviceIdType.MESH)
    lane = lax.broadcasted_iota(jnp.int32, (1, 128), 1)
    deep_y = 2 * (lane & 1) + (lane >> 6)
    ro, co = grid_of(32, 128)
    loads[0].wait()
    t2 = dot(w2_ref[...].reshape(27 * 16, 32), pick(ro == (co & 63) >> 1))
    ro, co = grid_of(16, 128)
    loads[1].wait()
    w1 = jnp.concatenate([w1_ref[k].astype(f32) for k in range(27)], axis=0).astype(bf16)
    t1 = dot(w1, pick(ro == (co & 15)))
    ro, co = grid_of(8, 128)
    near_y = 2 * ((co & 63) >> 4) + (co >> 6)
    taps_y = [jnp.where(ro == near_y + q - 1, 1.0, 0.0) for q in range(3)]

    def tap2(k):
        return t2[16 * k : 16 * k + 16]

    w1_rows, w2_rows = [], []
    for p in range(3):
        for r in range(3):
            for c in range(4):
                rows = [4 * (9 * p + 3 * q + r) + c for q in range(3)]
                w1_rows.append(sum(t1[k : k + 1] * taps_y[q] for q, k in enumerate(rows)))
            ks = [9 * p + 3 * q + r for q in range(3)]
            for y in range(4):
                w2_rows.append(sum(jnp.where(deep_y == y + 1 - q, tap2(k), 0.0) for q, k in enumerate(ks)))
    w1_wide = jnp.concatenate(w1_rows, axis=0).T.astype(bf16)
    w2_wide = jnp.concatenate(w2_rows, axis=0).T.astype(bf16)

    def taps_of(ref, i):
        return z_taps(ref[:, i].astype(f32).reshape(32, 128), 128)

    loads[2].wait()
    taps_own = [taps_of(vol_ref, i) for i in range(size_x)]

    pl.semaphore_wait(barrier, n_a - 1 + n_b - 1)

    right = {"space": jnp.minimum(s + 1, n_space - 1), "dp": d}
    left = {"space": jnp.maximum(s - 1, 0), "dp": d}

    def halo(src, dst, sem, to):
        return remote(src, dst, halo_send.at[sem], halo_recv.at[sem], to)

    to_right = [
        halo(vol_hbm.at[:, size_x - reach : size_x], vol_left, 0, right),
        halo(cot_hbm, cot_left, 1, right),
    ]
    to_left = [halo(vol_hbm.at[:, 0:reach], vol_right, 2, left), halo(cot_hbm, cot_right, 3, left)]

    @pl.when(outer)
    def _():
        for copy in to_right:
            copy.start()

    @pl.when(inner)
    def _():
        for copy in to_left:
            copy.start()

    def first_cols(taps):
        count = len(taps) - 2
        return jnp.concatenate([jnp.concatenate(taps[p : p + count], axis=1) for p in range(3)], axis=0)

    cols_mid = first_cols(taps_own)
    pre_mid = dot(w1_wide, cols_mid)
    sums_mid, slope_mid = halves(soft_terms(pre_mid)), slope_of(pre_mid)

    wb_cols = []
    for p in range(3):
        for r in range(3):
            ks = [26 - (9 * p + 3 * q + r) for q in range(3)]
            block = [
                sum(jnp.where(deep_y == y + q - 1, tap2(k), 0.0) for q, k in enumerate(ks)) for y in range(4)
            ]
            wb_cols.append(jnp.concatenate(block, axis=0))
    wb_wide = jnp.concatenate(wb_cols, axis=1).astype(bf16)
    loads[3].wait()
    loads[4].wait()

    @pl.when(outer)
    def _():
        for copy in to_right:
            copy.wait_send()
        for copy in to_left:
            copy.wait_recv()

    @pl.when(inner)
    def _():
        for copy in to_left:
            copy.wait_send()
        for copy in to_right:
            copy.wait_recv()

    taps_low = [taps_of(vol_left, i) for i in range(reach)] + taps_own[:2]
    taps_high = taps_own[-2:] + [taps_of(vol_right, i) for i in range(reach)]
    cols_low, cols_high = first_cols(taps_low), first_cols(taps_high)
    edge = 128 * (reach - 1)
    pre_low, pre_high = dot(w1_wide, cols_low), dot(w1_wide, cols_high)
    sums = [halves(soft_terms(pre_low)), sums_mid, halves(soft_terms(pre_high))]
    sum_x, sum_y = [jnp.concatenate(x, axis=1) for x in zip(*sums)]
    slope1 = jnp.concatenate([slope_of(pre_low[:, edge:]), slope_mid, slope_of(pre_high[:, :128])], axis=1)
    cols1 = jnp.concatenate([cols_low[:, edge:], cols_mid, cols_high[:, :128]], axis=1)
    pairs = []
    for j in range(4):
        pair = []
        for at in (512 * j, 512 * j + 256):
            x = sum_x[:, at : at + 128] + sum_x[:, at + 128 : at + 256]
            y = sum_y[:, at : at + 128] * sum_y[:, at + 128 : at + 256]
            pair.append(act_sum(x, y, 4))
        pairs.append(jnp.concatenate(pair, axis=1))
    pool = table_ref[at_pool1 : at_pool1 + 256]
    acts = dot(jnp.concatenate(pairs, axis=0).astype(bf16), pool).astype(bf16).astype(f32)
    even = [acts[64 * j : 64 * j + 64] for j in range(4)]
    even[0] = jnp.where(inner, even[0], 0.0)
    even[3] = jnp.where(outer, even[3], 0.0)
    odd = [between(even[j], even[j + 1]) for j in range(3)]

    even_taps = [z_taps(x, 64) for x in even]
    odd_taps = [z_taps(x, 64) for x in odd]
    cols2 = jnp.concatenate(
        [jnp.concatenate([even_taps[j], odd_taps[j], even_taps[j + 1]], axis=0) for j in range(3)], axis=1
    )
    pre2 = dot(w2_wide, cols2)
    slope2 = slope_of(pre2)

    def cot_rows(values):
        return values.astype(f32).reshape(64, 32)

    cots = [cot_left[:, deep_x - 1], cot_ref[:, 0], cot_ref[:, 1], cot_right[:, 0]]
    cots = jnp.concatenate([cot_rows(x) for x in cots], axis=1).astype(bf16)
    wide = [dot(cots, table_ref[at : at + 128]) for at in range(at_spread2, at_spread2 + 384, 128)]
    wide = jnp.concatenate(wide, axis=1)
    delta2 = (slope2 * jnp.concatenate([wide, wide], axis=0)).astype(bf16).astype(f32)
    row = lax.broadcasted_iota(jnp.int32, (128, 384), 1) >> 6
    own2 = jnp.where((row >= 1) & (row <= 4), delta2, 0.0).astype(bf16)

    grad2 = dot_lanes(cols2, own2)
    blocks = []
    for k in range(27):
        p, q, r = k // 9, k // 3 % 3, k % 3
        at = 64 * (3 * p + r)
        blocks.append(
            sum(jnp.where(deep_y == y + 1 - q, grad2[at + 16 * y : at + 16 * y + 16], 0.0) for y in range(4))
        )
    blocks.append(jnp.zeros((16, 128), f32))
    groups = [jnp.concatenate(blocks[7 * j : 7 * j + 7], axis=0) for j in range(4)]
    pay[0:112] = dot(jnp.concatenate(groups, axis=1).astype(bf16), table_ref[at_gather2 : at_gather2 + 512]).astype(bf16)
    if n_a * part > 112:
        pay[112:] = jnp.zeros((n_a * part - 112, 128), bf16)

    def rows_of(t):
        return pl.ds(pl.multiple_of(t * part, 16), part)

    parts = []
    for step in range(1, n_a):
        t, to = in_a(step)
        i = step - 1
        parts.append(remote(pay.at[rows_of(t)], got.at[i], rs_send.at[i], rs_recv.at[i], to))
        parts[-1].start()

    odd = [delta2[:, 128 * j : 128 * j + 128] for j in range(3)]
    odd_taps = [z_taps(x, 64) for x in odd]
    even_taps = [z_taps(between(odd[j], odd[j + 1]), 64) for j in range(2)]
    cols3 = jnp.concatenate(
        [jnp.concatenate([odd_taps[j], even_taps[j], odd_taps[j + 1]], axis=0) for j in range(2)], axis=1
    )
    back = dot(wb_wide, cols3).astype(bf16)
    spread = jnp.concatenate([table_ref[at : at + 128] for at in (at_spread1, at_spread1 + 128)], axis=1)
    wide = dot(jnp.concatenate([back[:, :128], back[:, 128:]], axis=0), spread)
    rows = [wide[64 * (i // 2) : 64 * (i // 2) + 64, 128 * (i % 2) : 128 * (i % 2) + 128] for i in range(4)]
    wide = jnp.concatenate([rows[i // 2] for i in range(8)], axis=1)
    delta1 = (slope1 * jnp.concatenate([wide, wide], axis=0)).astype(bf16)

    grad1 = dot_lanes(cols1, delta1).reshape(36, 8, 128)
    rows = [jnp.sum(grad1 * taps_y[q][None], axis=1) for q in range(3)]
    rows = jnp.concatenate(rows + [jnp.zeros((4, 128), f32)], axis=0)
    groups = jnp.concatenate([rows[16 * j : 16 * j + 16] for j in range(7)], axis=1)
    across[b, part:] = dot(groups.astype(bf16), table_ref[at_gather1 : at_gather1 + 896]).astype(bf16)

    total = pay[rows_of(a)].astype(f32)
    for i, copy in enumerate(parts):
        copy.wait_recv()
        total += got[i].astype(f32)
    across[b, :part] = total.astype(bf16)
    others = []
    for step in range(1, n_b):
        i, to = step - 1, in_b(step)[1]
        others.append(remote(across.at[b], across.at[b], ex_send.at[i], ex_recv.at[i], to))
        others[-1].start()
    act2 = act_sum(*halves(soft_terms(pre2)), 2).astype(bf16)
    out_ref[128:192] = dot(act2, table_ref[at_pool2 : at_pool2 + 384]).astype(bf16).astype(f32)
    for copy in parts:
        copy.wait_send()
    for copy in others:
        copy.wait()
    total = across[0].astype(f32)
    for i in range(1, n_b):
        total += across[i].astype(f32)

    full[a] = (total * (1.0 / n_dp)).astype(bf16)
    copies = []
    for step in range(1, n_a):
        i, to = step - 1, in_a(step)[1]
        copies.append(remote(full.at[a], full.at[a], ag_send.at[i], ag_recv.at[i], to))
        copies[-1].start()
    for copy in copies:
        copy.wait()
    for i in range(-(-112 // part)):
        rows = min(part, 112 - part * i)
        out_ref[part * i : part * i + rows] = full[i, :rows].astype(f32)
    total = full[0, part:].astype(f32)
    for i in range(1, n_a):
        total += full[i, part:].astype(f32)
    out_ref[112:128] = total


def unpack(in_ref, feat_hbm, g1_hbm, g2_hbm, feat_out, g1_out, g2_out, sems):
    for j in range(4):
        many = 7 if j < 3 else 6
        g2_out[7 * j : 7 * j + many] = in_ref[0 : 16 * many, 32 * j : 32 * j + 32].reshape(many, 16, 32)
    copies = [pltpu.make_async_copy(g2_out, g2_hbm, sems.at[0])]
    copies[0].start()
    for i in range(2):
        feat_out[:, i] = in_ref[128:192, 32 * i : 32 * i + 32].reshape(32, 2, 32).astype(bf16)
    copies.append(pltpu.make_async_copy(feat_out, feat_hbm, sems.at[1]))
    copies[1].start()
    for k in range(27):
        p, q, r = k // 9, k // 3 % 3, k % 3
        at = 36 * q + 4 * (3 * p + r)
        row, col = 112 + at % 16, 16 * (at // 16)
        g1_out[k] = in_ref[row : row + 4, col : col + 16]
    copies.append(pltpu.make_async_copy(g1_out, g1_hbm, sems.at[2]))
    copies[2].start()
    for copy in copies:
        copy.wait()


def shards(n_space, n_dp, volumes, first_kernel, middle_kernel, cotangent):
    n_a, n_b = 2 * n_space, n_dp // 2
    part = 16 * -(-112 // (16 * n_a))
    w1 = first_kernel.transpose(2, 3, 4, 1, 0).reshape(27, 4, 16)
    w2 = middle_kernel.transpose(2, 3, 4, 1, 0).reshape(27, 16, 32)
    cot = cotangent[0]
    vol = volumes[0]
    table = jnp.asarray(tables())
    halo = (vol.shape[0], reach) + vol.shape[2:]
    vmem = pl.BlockSpec(memory_space=pltpu.VMEM)
    hbm = pl.BlockSpec(memory_space=pltpu.HBM)
    dma = pltpu.SemaphoreType.DMA
    packed = pl.pallas_call(
        functools.partial(kernel, n_space, n_dp, part),
        out_shape=jax.ShapeDtypeStruct((192, 128), f32),
        in_specs=[hbm] * 5,
        out_specs=vmem,
        scratch_shapes=[
            pltpu.VMEM(vol.shape, bf16),
            pltpu.VMEM(w1.shape, bf16),
            pltpu.VMEM(w2.shape, bf16),
            pltpu.VMEM(cot.shape, bf16),
            pltpu.VMEM(halo, bf16),
            pltpu.VMEM(halo, bf16),
            pltpu.VMEM(cot.shape, bf16),
            pltpu.VMEM(cot.shape, bf16),
            pltpu.VMEM((n_a * part, 128), bf16),
            pltpu.VMEM((n_a - 1, part, 128), bf16),
            pltpu.VMEM((n_b, part + 16, 128), bf16),
            pltpu.VMEM((n_a, part + 16, 128), bf16),
            pltpu.VMEM(table.shape, bf16),
            dma((5,)),
            dma((4,)), dma((4,)),
            dma((n_a - 1,)), dma((n_a - 1,)),
            dma((max(n_b - 1, 1),)), dma((max(n_b - 1, 1),)),
            dma((n_a - 1,)), dma((n_a - 1,)),
        ],
        compiler_params=pltpu.CompilerParams(
            collective_id=0, has_side_effects=True, vmem_limit_bytes=24 * 1024 * 1024
        ),
        cost_estimate=pl.CostEstimate(flops=400_000_000, bytes_accessed=400_000, transcendentals=1_000_000),
    )(*[pltpu.with_memory_space_constraint(x, pltpu.HBM) for x in (vol, w1, w2, cot, table)])
    features, first_grad, middle_grad = pl.pallas_call(
        unpack,
        out_shape=(
            jax.ShapeDtypeStruct(cot.shape, bf16),
            jax.ShapeDtypeStruct((27, 4, 16), f32),
            jax.ShapeDtypeStruct((27, 16, 32), f32),
        ),
        in_specs=[vmem],
        out_specs=(hbm, hbm, hbm),
        scratch_shapes=[
            pltpu.VMEM(cot.shape, bf16),
            pltpu.VMEM((27, 4, 16), f32),
            pltpu.VMEM((27, 16, 32), f32),
            dma((3,)),
        ],
        compiler_params=pltpu.CompilerParams(vmem_limit_bytes=4 * 1024 * 1024),
    )(packed)
    first_grad = first_grad.reshape(3, 3, 3, 4, 16).transpose(4, 3, 0, 1, 2)
    middle_grad = middle_grad.reshape(3, 3, 3, 16, 32).transpose(4, 3, 0, 1, 2)
    return (features[None], first_grad, middle_grad)


def solution(mesh):
    in_specs = (P("dp", None, "space", None, None), P(), P(), P("dp", None, "space", None, None))
    out_specs = (P("dp", None, "space", None, None), P(), P())
    body = functools.partial(shards, mesh.shape["space"], mesh.shape["dp"])
    return jax.shard_map(body, mesh=mesh, in_specs=in_specs, out_specs=out_specs, check_vma=False)
```

```python
import functools
import math

import jax
import jax.numpy as jnp
import numpy as np
from jax import lax
from jax.experimental import pallas as pl
from jax.experimental.pallas import tpu as pltpu
from jax.sharding import PartitionSpec as P

leak_slope = 0.3
soft_share = 0.7
log_two = math.log(2.0)
reach = 5
f32, bf16 = jnp.float32, jnp.bfloat16


def soft_terms(a):
    return jnp.maximum(leak_slope * a, a), 1.0 + jnp.exp(-jnp.abs(a))


def halves(terms):
    x, y = terms
    return x[:64] + x[64:], y[:64] * y[64:]


def act_sum(x, y, count):
    return x + soft_share * (jnp.log(y) - count * log_two)


def slope_of(a):
    return (leak_slope + 0.5 * soft_share) + 0.5 * soft_share * jnp.tanh(0.5 * a)


def dot(a, b):
    return jnp.dot(a, b, preferred_element_type=f32)


def dot_lanes(a, b):
    return lax.dot_general(a, b, (((1,), (1,)), ((), ())), preferred_element_type=f32)


def grid_of(rows, cols):
    return (
        lax.broadcasted_iota(jnp.int32, (rows, cols), 0),
        lax.broadcasted_iota(jnp.int32, (rows, cols), 1),
    )


def pick(where, value=1.0):
    return jnp.where(where, value, 0.0).astype(bf16)


def tables():
    def table(rows, cols, rule):
        return rule(np.arange(rows)[:, None], np.arange(cols)[None, :])

    pool1 = table(256, 128, lambda r, c: (r >> 7 == c >> 6) & ((r & 127) >> 1 == (c & 63))) * 0.125
    row = (np.arange(384) >> 6)[:, None]
    pool2 = table(384, 128, lambda r, c: ((r & 63) >> 1 == (c & 31)) & (c < 64) & ((row - 1) >> 1 == c >> 5))
    pool2 = pool2 * 0.125 * ((row >= 1) & (row <= 4))
    spread1 = table(128, 256, lambda r, c: (r >> 6 == c >> 7) & ((r & 63) == (c & 127) >> 1)) * 0.125
    spread2 = table(128, 384, lambda r, c: (((c >> 6) + 1) >> 1 == r >> 5) & ((c & 63) >> 1 == (r & 31))) * 0.125
    gather1 = table(896, 128, lambda r, c: (r >> 7 == c >> 4) & ((r & 15) == (c & 15)))
    gather2 = table(512, 128, lambda r, c: (r >> 7 == c >> 5) & ((r & 63) >> 1 == (c & 31)))
    parts = [pool1, pool2, *np.split(spread1, 2, 1), *np.split(spread2, 3, 1), gather1, gather2]
    return np.concatenate(parts, 0).astype(np.float32).astype(bf16)


at_pool1, at_pool2, at_spread1, at_spread2, at_gather1, at_gather2 = 0, 256, 640, 896, 1280, 2176


def z_taps(a, width):
    place = lax.broadcasted_iota(jnp.int32, a.shape, 1) & (width - 1)
    before = jnp.where(place == 0, 0.0, pltpu.roll(a, 1, 1))
    after = jnp.where(place == width - 1, 0.0, pltpu.roll(a, 127, 1))
    return jnp.concatenate([before, a, after], axis=0).astype(bf16)


def between(a, b):
    place = lax.broadcasted_iota(jnp.int32, a.shape, 1)
    return jnp.where(place < 64, pltpu.roll(a, 64, 1), pltpu.roll(b, 64, 1))


def remote(src, dst, send, recv, to):
    return pltpu.make_async_remote_copy(
        src_ref=src, dst_ref=dst, send_sem=send, recv_sem=recv, device_id=to, device_id_type=pl.DeviceIdType.MESH
    )


def kernel(
    n_space, n_dp, part,
    vol_hbm, w1_hbm, w2_hbm, cot_hbm, table_hbm,
    out_ref,
    vol_ref, w1_ref, w2_ref, cot_ref, vol_left, vol_right, cot_left, cot_right, pay, got, across, full,
    table_ref,
    load, halo_send, halo_recv, rs_send, rs_recv, ex_send, ex_recv, ag_send, ag_recv,
):
    s, d = lax.axis_index("space"), lax.axis_index("dp")
    n_a, n_b = 2 * n_space, n_dp // 2
    a, b = 2 * s + lax.rem(d, 2), d // 2
    inner = s > 0
    outer = s < n_space - 1

    def in_a(step):
        t = lax.rem(a + step, n_a)
        return t, {"space": t // 2, "dp": 2 * b + lax.rem(t, 2)}

    def in_b(step):
        t = lax.rem(b + step, n_b)
        return t, {"space": s, "dp": 2 * t + lax.rem(d, 2)}

    barrier = pltpu.get_barrier_semaphore()
    for step in sorted(range(1, n_a), key=lambda step: abs(min(step, n_a - step) - 2)):
        pl.semaphore_signal(barrier, inc=1, device_id=in_a(step)[1], device_id_type=pl.DeviceIdType.MESH)
    for step in range(1, n_b):
        pl.semaphore_signal(barrier, inc=1, device_id=in_b(step)[1], device_id_type=pl.DeviceIdType.MESH)
    loads = [
        pltpu.make_async_copy(src, dst, load.at[i])
        for i, (src, dst) in enumerate(
            [(w2_hbm, w2_ref), (w1_hbm, w1_ref), (vol_hbm, vol_ref), (cot_hbm, cot_ref), (table_hbm, table_ref)]
        )
    ]
    for copy in loads:
        copy.start()

    @pl.when(jnp.logical_not(inner))
    def _():
        vol_left[...] = jnp.zeros_like(vol_left)
        cot_left[...] = jnp.zeros_like(cot_left)

    @pl.when(jnp.logical_not(outer))
    def _():
        vol_right[...] = jnp.zeros_like(vol_right)
        cot_right[...] = jnp.zeros_like(cot_right)

    pl.semaphore_wait(barrier, n_a - 1 + n_b - 1)

    right = {"space": jnp.minimum(s + 1, n_space - 1), "dp": d}
    left = {"space": jnp.maximum(s - 1, 0), "dp": d}
    size_x = vol_hbm.shape[1]
    deep_x = cot_hbm.shape[1]

    def halo(src, dst, sem, to):
        return remote(src, dst, halo_send.at[sem], halo_recv.at[sem], to)

    to_right = [
        halo(vol_hbm.at[:, size_x - reach : size_x], vol_left, 0, right),
        halo(cot_hbm.at[:, deep_x - 1], cot_left, 1, right),
    ]
    to_left = [halo(vol_hbm.at[:, 0:reach], vol_right, 2, left), halo(cot_hbm.at[:, 0], cot_right, 3, left)]

    @pl.when(outer)
    def _():
        for copy in to_right:
            copy.start()

    @pl.when(inner)
    def _():
        for copy in to_left:
            copy.start()

    lane = lax.broadcasted_iota(jnp.int32, (1, 128), 1)
    deep_y = 2 * (lane & 1) + (lane >> 6)
    ro, co = grid_of(32, 128)
    loads[0].wait()
    t2 = dot(w2_ref[...].reshape(27 * 16, 32), pick(ro == (co & 63) >> 1))
    ro, co = grid_of(16, 128)
    loads[1].wait()
    w1 = jnp.concatenate([w1_ref[k].astype(f32) for k in range(27)], axis=0).astype(bf16)
    t1 = dot(w1, pick(ro == (co & 15)))
    ro, co = grid_of(8, 128)
    near_y = 2 * ((co & 63) >> 4) + (co >> 6)
    taps_y = [jnp.where(ro == near_y + q - 1, 1.0, 0.0) for q in range(3)]

    def tap2(k):
        return t2[16 * k : 16 * k + 16]

    w1_rows, w2_rows, wb_cols = [], [], []
    for p in range(3):
        for r in range(3):
            for c in range(4):
                rows = [4 * (9 * p + 3 * q + r) + c for q in range(3)]
                w1_rows.append(sum(t1[k : k + 1] * taps_y[q] for q, k in enumerate(rows)))
            ks = [9 * p + 3 * q + r for q in range(3)]
            block = []
            for y in range(4):
                w2_rows.append(sum(jnp.where(deep_y == y + 1 - q, tap2(k), 0.0) for q, k in enumerate(ks)))
                block.append(sum(jnp.where(deep_y == y + q - 1, tap2(26 - k), 0.0) for q, k in enumerate(ks)))
            wb_cols.append(jnp.concatenate(block, axis=0))
    w1_wide = jnp.concatenate(w1_rows, axis=0).T.astype(bf16)
    w2_wide = jnp.concatenate(w2_rows, axis=0).T.astype(bf16)
    wb_wide = jnp.concatenate(wb_cols, axis=1).astype(bf16)

    def taps_of(ref, i):
        return z_taps(ref[:, i].astype(f32).reshape(32, 128), 128)

    def first_cols(taps):
        count = len(taps) - 2
        return jnp.concatenate([jnp.concatenate(taps[p : p + count], axis=1) for p in range(3)], axis=0)

    loads[2].wait()
    taps_own = [taps_of(vol_ref, i) for i in range(size_x)]
    cols_mid = first_cols(taps_own)
    pre_mid = dot(w1_wide, cols_mid)
    sums_mid, slope_mid = halves(soft_terms(pre_mid)), slope_of(pre_mid)

    def halo_wait(i):
        @pl.when(outer)
        def _():
            to_right[i].wait_send()
            to_left[i].wait_recv()

        @pl.when(inner)
        def _():
            to_left[i].wait_send()
            to_right[i].wait_recv()

    halo_wait(0)

    taps_low = [taps_of(vol_left, i) for i in range(reach)] + taps_own[:2]
    taps_high = taps_own[-2:] + [taps_of(vol_right, i) for i in range(reach)]
    cols_low, cols_high = first_cols(taps_low), first_cols(taps_high)
    edge = 128 * (reach - 1)
    pre_low, pre_high = dot(w1_wide, cols_low), dot(w1_wide, cols_high)
    sums = [halves(soft_terms(pre_low)), sums_mid, halves(soft_terms(pre_high))]
    sum_x, sum_y = [jnp.concatenate(x, axis=1) for x in zip(*sums)]
    slope1 = jnp.concatenate([slope_of(pre_low[:, edge:]), slope_mid, slope_of(pre_high[:, :128])], axis=1)
    cols1 = jnp.concatenate([cols_low[:, edge:], cols_mid, cols_high[:, :128]], axis=1)
    pairs = []
    for j in range(4):
        pair = []
        for at in (512 * j, 512 * j + 256):
            x = sum_x[:, at : at + 128] + sum_x[:, at + 128 : at + 256]
            y = sum_y[:, at : at + 128] * sum_y[:, at + 128 : at + 256]
            pair.append(act_sum(x, y, 4))
        pairs.append(jnp.concatenate(pair, axis=1))
    loads[4].wait()
    pool = table_ref[at_pool1 : at_pool1 + 256]
    acts = dot(jnp.concatenate(pairs, axis=0).astype(bf16), pool).astype(bf16).astype(f32)
    even = [acts[64 * j : 64 * j + 64] for j in range(4)]
    even[0] = jnp.where(inner, even[0], 0.0)
    even[3] = jnp.where(outer, even[3], 0.0)
    odd = [between(even[j], even[j + 1]) for j in range(3)]

    even_taps = [z_taps(x, 64) for x in even]
    odd_taps = [z_taps(x, 64) for x in odd]
    cols2 = jnp.concatenate(
        [jnp.concatenate([even_taps[j], odd_taps[j], even_taps[j + 1]], axis=0) for j in range(3)], axis=1
    )
    pre2 = dot(w2_wide, cols2)
    slope2 = slope_of(pre2)

    def cot_rows(values):
        return values.astype(f32).reshape(64, 32)

    loads[3].wait()
    halo_wait(1)
    cots = [cot_left[...], cot_ref[:, 0], cot_ref[:, 1], cot_right[...]]
    cots = jnp.concatenate([cot_rows(x) for x in cots], axis=1).astype(bf16)
    wide = [dot(cots, table_ref[at : at + 128]) for at in range(at_spread2, at_spread2 + 384, 128)]
    wide = jnp.concatenate(wide, axis=1)
    delta2 = (slope2 * jnp.concatenate([wide, wide], axis=0)).astype(bf16).astype(f32)
    row = lax.broadcasted_iota(jnp.int32, (128, 384), 1) >> 6
    own2 = jnp.where((row >= 1) & (row <= 4), delta2, 0.0).astype(bf16)

    grad2 = dot_lanes(cols2, own2)
    blocks = []
    for k in range(27):
        p, q, r = k // 9, k // 3 % 3, k % 3
        at = 64 * (3 * p + r)
        blocks.append(
            sum(jnp.where(deep_y == y + 1 - q, grad2[at + 16 * y : at + 16 * y + 16], 0.0) for y in range(4))
        )
    blocks.append(jnp.zeros((16, 128), f32))
    groups = [jnp.concatenate(blocks[7 * j : 7 * j + 7], axis=0) for j in range(4)]
    pay[0:112] = dot(jnp.concatenate(groups, axis=1).astype(bf16), table_ref[at_gather2 : at_gather2 + 512]).astype(bf16)
    if n_a * part > 112:
        pay[112:] = jnp.zeros((n_a * part - 112, 128), bf16)

    def rows_of(t):
        return pl.ds(pl.multiple_of(t * part, 16), part)

    parts = []
    for step in range(1, n_a):
        t, to = in_a(step)
        i = step - 1
        parts.append(remote(pay.at[rows_of(t)], got.at[i], rs_send.at[i], rs_recv.at[i], to))
        parts[-1].start()

    odd = [delta2[:, 128 * j : 128 * j + 128] for j in range(3)]
    odd_taps = [z_taps(x, 64) for x in odd]
    even_taps = [z_taps(between(odd[j], odd[j + 1]), 64) for j in range(2)]
    cols3 = jnp.concatenate(
        [jnp.concatenate([odd_taps[j], even_taps[j], odd_taps[j + 1]], axis=0) for j in range(2)], axis=1
    )
    back = dot(wb_wide, cols3).astype(bf16)
    spread = jnp.concatenate([table_ref[at : at + 128] for at in (at_spread1, at_spread1 + 128)], axis=1)
    wide = dot(jnp.concatenate([back[:, :128], back[:, 128:]], axis=0), spread)
    rows = [wide[64 * (i // 2) : 64 * (i // 2) + 64, 128 * (i % 2) : 128 * (i % 2) + 128] for i in range(4)]
    wide = jnp.concatenate([rows[i // 2] for i in range(8)], axis=1)
    delta1 = (slope1 * jnp.concatenate([wide, wide], axis=0)).astype(bf16)

    grad1 = dot_lanes(cols1, delta1).reshape(36, 8, 128)
    rows = [jnp.sum(grad1 * taps_y[q][None], axis=1) for q in range(3)]
    rows = jnp.concatenate(rows + [jnp.zeros((4, 128), f32)], axis=0)
    groups = jnp.concatenate([rows[16 * j : 16 * j + 16] for j in range(7)], axis=1)
    across[b, part:] = dot(groups.astype(bf16), table_ref[at_gather1 : at_gather1 + 896]).astype(bf16)

    total = pay[rows_of(a)].astype(f32)
    for i, copy in enumerate(parts):
        copy.wait_recv()
        total += got[i].astype(f32)
    across[b, :part] = total.astype(bf16)
    others = []
    for step in range(1, n_b):
        i, to = step - 1, in_b(step)[1]
        others.append(remote(across.at[b], across.at[b], ex_send.at[i], ex_recv.at[i], to))
        others[-1].start()
    act2 = act_sum(*halves(soft_terms(pre2)), 2).astype(bf16)
    out_ref[128:192] = dot(act2, table_ref[at_pool2 : at_pool2 + 384]).astype(bf16).astype(f32)
    for copy in parts:
        copy.wait_send()
    for copy in others:
        copy.wait()
    total = across[0].astype(f32)
    for i in range(1, n_b):
        total += across[i].astype(f32)

    full[a] = (total * (1.0 / n_dp)).astype(bf16)
    copies = []
    for step in range(1, n_a):
        i, to = step - 1, in_a(step)[1]
        copies.append(remote(full.at[a], full.at[a], ag_send.at[i], ag_recv.at[i], to))
        copies[-1].start()
    for copy in copies:
        copy.wait()
    for i in range(-(-112 // part)):
        rows = min(part, 112 - part * i)
        out_ref[part * i : part * i + rows] = full[i, :rows].astype(f32)
    total = full[0, part:].astype(f32)
    for i in range(1, n_a):
        total += full[i, part:].astype(f32)
    out_ref[112:128] = total


def unpack(in_ref, feat_hbm, g1_hbm, g2_hbm, feat_out, g1_out, g2_out, sems):
    for j in range(4):
        many = 7 if j < 3 else 6
        g2_out[7 * j : 7 * j + many] = in_ref[0 : 16 * many, 32 * j : 32 * j + 32].reshape(many, 16, 32)
    copies = [pltpu.make_async_copy(g2_out, g2_hbm, sems.at[0])]
    copies[0].start()
    for i in range(2):
        feat_out[:, i] = in_ref[128:192, 32 * i : 32 * i + 32].reshape(32, 2, 32).astype(bf16)
    copies.append(pltpu.make_async_copy(feat_out, feat_hbm, sems.at[1]))
    copies[1].start()
    for k in range(27):
        p, q, r = k // 9, k // 3 % 3, k % 3
        at = 36 * q + 4 * (3 * p + r)
        row, col = 112 + at % 16, 16 * (at // 16)
        g1_out[k] = in_ref[row : row + 4, col : col + 16]
    copies.append(pltpu.make_async_copy(g1_out, g1_hbm, sems.at[2]))
    copies[2].start()
    for copy in copies:
        copy.wait()


def shards(n_space, n_dp, volumes, first_kernel, middle_kernel, cotangent):
    n_a, n_b = 2 * n_space, n_dp // 2
    part = 16 * -(-112 // (16 * n_a))
    w1 = first_kernel.transpose(2, 3, 4, 1, 0).reshape(27, 4, 16)
    w2 = middle_kernel.transpose(2, 3, 4, 1, 0).reshape(27, 16, 32)
    cot = cotangent[0]
    vol = volumes[0]
    table = jnp.asarray(tables())
    halo = (vol.shape[0], reach) + vol.shape[2:]
    edge = (cot.shape[0],) + cot.shape[2:]
    vmem = pl.BlockSpec(memory_space=pltpu.VMEM)
    hbm = pl.BlockSpec(memory_space=pltpu.HBM)
    dma = pltpu.SemaphoreType.DMA
    packed = pl.pallas_call(
        functools.partial(kernel, n_space, n_dp, part),
        out_shape=jax.ShapeDtypeStruct((192, 128), f32),
        in_specs=[hbm] * 5,
        out_specs=vmem,
        scratch_shapes=[
            pltpu.VMEM(vol.shape, bf16),
            pltpu.VMEM(w1.shape, bf16),
            pltpu.VMEM(w2.shape, bf16),
            pltpu.VMEM(cot.shape, bf16),
            pltpu.VMEM(halo, bf16),
            pltpu.VMEM(halo, bf16),
            pltpu.VMEM(edge, bf16),
            pltpu.VMEM(edge, bf16),
            pltpu.VMEM((n_a * part, 128), bf16),
            pltpu.VMEM((n_a - 1, part, 128), bf16),
            pltpu.VMEM((n_b, part + 16, 128), bf16),
            pltpu.VMEM((n_a, part + 16, 128), bf16),
            pltpu.VMEM(table.shape, bf16),
            dma((5,)),
            dma((4,)), dma((4,)),
            dma((n_a - 1,)), dma((n_a - 1,)),
            dma((max(n_b - 1, 1),)), dma((max(n_b - 1, 1),)),
            dma((n_a - 1,)), dma((n_a - 1,)),
        ],
        compiler_params=pltpu.CompilerParams(
            collective_id=0, has_side_effects=True, vmem_limit_bytes=24 * 1024 * 1024
        ),
        cost_estimate=pl.CostEstimate(flops=400_000_000, bytes_accessed=400_000, transcendentals=1_000_000),
    )(*[pltpu.with_memory_space_constraint(x, pltpu.HBM) for x in (vol, w1, w2, cot, table)])
    features, first_grad, middle_grad = pl.pallas_call(
        unpack,
        out_shape=(
            jax.ShapeDtypeStruct(cot.shape, bf16),
            jax.ShapeDtypeStruct((27, 4, 16), f32),
            jax.ShapeDtypeStruct((27, 16, 32), f32),
        ),
        in_specs=[vmem],
        out_specs=(hbm, hbm, hbm),
        scratch_shapes=[
            pltpu.VMEM(cot.shape, bf16),
            pltpu.VMEM((27, 4, 16), f32),
            pltpu.VMEM((27, 16, 32), f32),
            dma((3,)),
        ],
        compiler_params=pltpu.CompilerParams(vmem_limit_bytes=4 * 1024 * 1024),
    )(packed)
    first_grad = first_grad.reshape(3, 3, 3, 4, 16).transpose(4, 3, 0, 1, 2)
    middle_grad = middle_grad.reshape(3, 3, 3, 16, 32).transpose(4, 3, 0, 1, 2)
    return (features[None], first_grad, middle_grad)


def solution(mesh):
    in_specs = (P("dp", None, "space", None, None), P(), P(), P("dp", None, "space", None, None))
    out_specs = (P("dp", None, "space", None, None), P(), P())
    body = functools.partial(shards, mesh.shape["space"], mesh.shape["dp"])
    return jax.shard_map(body, mesh=mesh, in_specs=in_specs, out_specs=out_specs, check_vma=False)
```

```python
import functools
import math

import jax
import jax.numpy as jnp
import numpy as np
from jax import lax
from jax.experimental import pallas as pl
from jax.experimental.pallas import tpu as pltpu
from jax.sharding import PartitionSpec as P

leak_slope = 0.3
soft_share = 0.7
log_two = math.log(2.0)
reach = 5
f32, bf16 = jnp.float32, jnp.bfloat16


def soft_terms(a):
    return jnp.maximum(leak_slope * a, a), 1.0 + jnp.exp(-jnp.abs(a))


def halves(terms):
    x, y = terms
    return x[:64] + x[64:], y[:64] * y[64:]


def act_sum(x, y, count):
    return x + soft_share * (jnp.log(y) - count * log_two)


def slope_of(a):
    return (leak_slope + 0.5 * soft_share) + 0.5 * soft_share * jnp.tanh(0.5 * a)


def dot(a, b):
    return jnp.dot(a, b, preferred_element_type=f32)


def dot_lanes(a, b):
    return lax.dot_general(a, b, (((1,), (1,)), ((), ())), preferred_element_type=f32)


def grid_of(rows, cols):
    return (
        lax.broadcasted_iota(jnp.int32, (rows, cols), 0),
        lax.broadcasted_iota(jnp.int32, (rows, cols), 1),
    )


def pick(where, value=1.0):
    return jnp.where(where, value, 0.0).astype(bf16)


def tables():
    def table(rows, cols, rule):
        return rule(np.arange(rows)[:, None], np.arange(cols)[None, :])

    pool1 = table(256, 128, lambda r, c: (r >> 7 == c >> 6) & ((r & 127) >> 1 == (c & 63))) * 0.125
    row = (np.arange(384) >> 6)[:, None]
    pool2 = table(384, 128, lambda r, c: ((r & 63) >> 1 == (c & 31)) & (c < 64) & ((row - 1) >> 1 == c >> 5))
    pool2 = pool2 * 0.125 * ((row >= 1) & (row <= 4))
    spread1 = table(128, 256, lambda r, c: (r >> 6 == c >> 7) & ((r & 63) == (c & 127) >> 1)) * 0.125
    spread2 = table(128, 384, lambda r, c: (((c >> 6) + 1) >> 1 == r >> 5) & ((c & 63) >> 1 == (r & 31))) * 0.125
    gather1 = table(896, 128, lambda r, c: (r >> 7 == c >> 4) & ((r & 15) == (c & 15)))
    gather2 = table(512, 128, lambda r, c: (r >> 7 == c >> 5) & ((r & 63) >> 1 == (c & 31)))
    parts = [pool1, pool2, *np.split(spread1, 2, 1), *np.split(spread2, 3, 1), gather1, gather2]
    return np.concatenate(parts, 0).astype(np.float32).astype(bf16)


at_pool1, at_pool2, at_spread1, at_spread2, at_gather1, at_gather2 = 0, 256, 640, 896, 1280, 2176


def z_taps(a, width):
    place = lax.broadcasted_iota(jnp.int32, a.shape, 1) & (width - 1)
    before = jnp.where(place == 0, 0.0, pltpu.roll(a, 1, 1))
    after = jnp.where(place == width - 1, 0.0, pltpu.roll(a, 127, 1))
    return jnp.concatenate([before, a, after], axis=0).astype(bf16)


def between(a, b):
    place = lax.broadcasted_iota(jnp.int32, a.shape, 1)
    return jnp.where(place < 64, pltpu.roll(a, 64, 1), pltpu.roll(b, 64, 1))


def remote(src, dst, send, recv, to):
    return pltpu.make_async_remote_copy(
        src_ref=src, dst_ref=dst, send_sem=send, recv_sem=recv, device_id=to, device_id_type=pl.DeviceIdType.MESH
    )


def kernel(
    n_space, n_dp, part,
    vol_hbm, w1_hbm, w2_hbm, cot_hbm, table_hbm,
    out_ref,
    vol_ref, w1_ref, w2_ref, cot_ref, vol_left, vol_right, cot_left, cot_right, pay, got, across, full,
    table_ref,
    load, halo_send, halo_recv, rs_send, rs_recv, ex_send, ex_recv, ag_send, ag_recv,
):
    s, d = lax.axis_index("space"), lax.axis_index("dp")
    n_a, n_b = 2 * n_space, n_dp // 2
    a, b = 2 * s + lax.rem(d, 2), d // 2
    inner = s > 0
    outer = s < n_space - 1

    def in_a(step):
        t = lax.rem(a + step, n_a)
        return t, {"space": t // 2, "dp": 2 * b + lax.rem(t, 2)}

    def in_b(step):
        t = lax.rem(b + step, n_b)
        return t, {"space": s, "dp": 2 * t + lax.rem(d, 2)}

    loads = [
        pltpu.make_async_copy(src, dst, load.at[i])
        for i, (src, dst) in enumerate(
            [(w2_hbm, w2_ref), (w1_hbm, w1_ref), (vol_hbm, vol_ref), (cot_hbm, cot_ref), (table_hbm, table_ref)]
        )
    ]
    for copy in loads[:4]:
        copy.start()
    for ref in (vol_left, vol_right, cot_left, cot_right):
        ref[...] = jnp.zeros_like(ref)
    barrier = pltpu.get_barrier_semaphore()
    for step in range(1, n_a):
        pl.semaphore_signal(barrier, inc=1, device_id=in_a(step)[1], device_id_type=pl.DeviceIdType.MESH)
    for step in range(1, n_b):
        pl.semaphore_signal(barrier, inc=1, device_id=in_b(step)[1], device_id_type=pl.DeviceIdType.MESH)
    pl.semaphore_wait(barrier, n_a - 1 + n_b - 1)

    right = {"space": jnp.minimum(s + 1, n_space - 1), "dp": d}
    left = {"space": jnp.maximum(s - 1, 0), "dp": d}
    size_x = vol_hbm.shape[1]
    deep_x = cot_hbm.shape[1]

    def halo(src, dst, sem, to):
        return remote(src, dst, halo_send.at[sem], halo_recv.at[sem], to)

    to_right = [
        halo(vol_hbm.at[:, size_x - reach : size_x], vol_left, 0, right),
        halo(cot_hbm.at[:, deep_x - 1], cot_left, 1, right),
    ]
    to_left = [halo(vol_hbm.at[:, 0:reach], vol_right, 2, left), halo(cot_hbm.at[:, 0], cot_right, 3, left)]

    @pl.when(outer)
    def _():
        for copy in to_right:
            copy.start()

    @pl.when(inner)
    def _():
        for copy in to_left:
            copy.start()

    loads[4].start()

    lane = lax.broadcasted_iota(jnp.int32, (1, 128), 1)
    deep_y = 2 * (lane & 1) + (lane >> 6)
    ro, co = grid_of(32, 128)
    loads[0].wait()
    t2 = dot(w2_ref[...].reshape(27 * 16, 32), pick(ro == (co & 63) >> 1))
    ro, co = grid_of(16, 128)
    loads[1].wait()
    w1 = jnp.concatenate([w1_ref[k].astype(f32) for k in range(27)], axis=0).astype(bf16)
    t1 = dot(w1, pick(ro == (co & 15)))
    ro, co = grid_of(8, 128)
    near_y = 2 * ((co & 63) >> 4) + (co >> 6)
    taps_y = [jnp.where(ro == near_y + q - 1, 1.0, 0.0) for q in range(3)]

    def tap2(k):
        return t2[16 * k : 16 * k + 16]

    w1_rows, w2_rows, wb_cols = [], [], []
    for p in range(3):
        for r in range(3):
            for c in range(4):
                rows = [4 * (9 * p + 3 * q + r) + c for q in range(3)]
                w1_rows.append(sum(t1[k : k + 1] * taps_y[q] for q, k in enumerate(rows)))
            ks = [9 * p + 3 * q + r for q in range(3)]
            block = []
            for y in range(4):
                w2_rows.append(sum(jnp.where(deep_y == y + 1 - q, tap2(k), 0.0) for q, k in enumerate(ks)))
                block.append(sum(jnp.where(deep_y == y + q - 1, tap2(26 - k), 0.0) for q, k in enumerate(ks)))
            wb_cols.append(jnp.concatenate(block, axis=0))
    w1_wide = jnp.concatenate(w1_rows, axis=0).T.astype(bf16)
    w2_wide = jnp.concatenate(w2_rows, axis=0).T.astype(bf16)
    wb_wide = jnp.concatenate(wb_cols, axis=1).astype(bf16)

    def taps_of(ref, i):
        return z_taps(ref[:, i].astype(f32).reshape(32, 128), 128)

    def first_cols(taps):
        count = len(taps) - 2
        return jnp.concatenate([jnp.concatenate(taps[p : p + count], axis=1) for p in range(3)], axis=0)

    loads[2].wait()
    taps_own = [taps_of(vol_ref, i) for i in range(size_x)]
    cols_mid = first_cols(taps_own)
    pre_mid = dot(w1_wide, cols_mid)
    sums_mid, slope_mid = halves(soft_terms(pre_mid)), slope_of(pre_mid)

    loads[3].wait()
    loads[4].wait()

    @pl.when(outer)
    def _():
        for copy in to_right:
            copy.wait_send()
        for copy in to_left:
            copy.wait_recv()

    @pl.when(inner)
    def _():
        for copy in to_left:
            copy.wait_send()
        for copy in to_right:
            copy.wait_recv()

    taps_low = [taps_of(vol_left, i) for i in range(reach)] + taps_own[:2]
    taps_high = taps_own[-2:] + [taps_of(vol_right, i) for i in range(reach)]
    cols_low, cols_high = first_cols(taps_low), first_cols(taps_high)
    edge = 128 * (reach - 1)
    pre_low, pre_high = dot(w1_wide, cols_low), dot(w1_wide, cols_high)
    sums = [halves(soft_terms(pre_low)), sums_mid, halves(soft_terms(pre_high))]
    sum_x, sum_y = [jnp.concatenate(x, axis=1) for x in zip(*sums)]
    slope1 = jnp.concatenate([slope_of(pre_low[:, edge:]), slope_mid, slope_of(pre_high[:, :128])], axis=1)
    cols1 = jnp.concatenate([cols_low[:, edge:], cols_mid, cols_high[:, :128]], axis=1)
    pairs = []
    for j in range(4):
        pair = []
        for at in (512 * j, 512 * j + 256):
            x = sum_x[:, at : at + 128] + sum_x[:, at + 128 : at + 256]
            y = sum_y[:, at : at + 128] * sum_y[:, at + 128 : at + 256]
            pair.append(act_sum(x, y, 4))
        pairs.append(jnp.concatenate(pair, axis=1))
    pool = table_ref[at_pool1 : at_pool1 + 256]
    acts = dot(jnp.concatenate(pairs, axis=0).astype(bf16), pool).astype(bf16).astype(f32)
    even = [acts[64 * j : 64 * j + 64] for j in range(4)]
    even[0] = jnp.where(inner, even[0], 0.0)
    even[3] = jnp.where(outer, even[3], 0.0)
    odd = [between(even[j], even[j + 1]) for j in range(3)]

    even_taps = [z_taps(x, 64) for x in even]
    odd_taps = [z_taps(x, 64) for x in odd]
    cols2 = jnp.concatenate(
        [jnp.concatenate([even_taps[j], odd_taps[j], even_taps[j + 1]], axis=0) for j in range(3)], axis=1
    )
    pre2 = dot(w2_wide, cols2)
    slope2 = slope_of(pre2)

    def cot_rows(values):
        return values.astype(f32).reshape(64, 32)

    cots = [cot_left[...], cot_ref[:, 0], cot_ref[:, 1], cot_right[...]]
    cots = jnp.concatenate([cot_rows(x) for x in cots], axis=1).astype(bf16)
    wide = [dot(cots, table_ref[at : at + 128]) for at in range(at_spread2, at_spread2 + 384, 128)]
    wide = jnp.concatenate(wide, axis=1)
    delta2 = (slope2 * jnp.concatenate([wide, wide], axis=0)).astype(bf16).astype(f32)
    row = lax.broadcasted_iota(jnp.int32, (128, 384), 1) >> 6
    own2 = jnp.where((row >= 1) & (row <= 4), delta2, 0.0).astype(bf16)

    grad2 = dot_lanes(cols2, own2)
    blocks = []
    for k in range(27):
        p, q, r = k // 9, k // 3 % 3, k % 3
        at = 64 * (3 * p + r)
        blocks.append(
            sum(jnp.where(deep_y == y + 1 - q, grad2[at + 16 * y : at + 16 * y + 16], 0.0) for y in range(4))
        )
    blocks.append(jnp.zeros((16, 128), f32))
    groups = [jnp.concatenate(blocks[7 * j : 7 * j + 7], axis=0) for j in range(4)]
    pay[0:112] = dot(jnp.concatenate(groups, axis=1).astype(bf16), table_ref[at_gather2 : at_gather2 + 512]).astype(bf16)
    if n_a * part > 112:
        pay[112:] = jnp.zeros((n_a * part - 112, 128), bf16)

    def rows_of(t):
        return pl.ds(pl.multiple_of(t * part, 16), part)

    parts = []
    for step in range(1, n_a):
        t, to = in_a(step)
        i = step - 1
        parts.append(remote(pay.at[rows_of(t)], got.at[i], rs_send.at[i], rs_recv.at[i], to))
        parts[-1].start()

    odd = [delta2[:, 128 * j : 128 * j + 128] for j in range(3)]
    odd_taps = [z_taps(x, 64) for x in odd]
    even_taps = [z_taps(between(odd[j], odd[j + 1]), 64) for j in range(2)]
    cols3 = jnp.concatenate(
        [jnp.concatenate([odd_taps[j], even_taps[j], odd_taps[j + 1]], axis=0) for j in range(2)], axis=1
    )
    back = dot(wb_wide, cols3).astype(bf16)
    spread = jnp.concatenate([table_ref[at : at + 128] for at in (at_spread1, at_spread1 + 128)], axis=1)
    wide = dot(jnp.concatenate([back[:, :128], back[:, 128:]], axis=0), spread)
    rows = [wide[64 * (i // 2) : 64 * (i // 2) + 64, 128 * (i % 2) : 128 * (i % 2) + 128] for i in range(4)]
    wide = jnp.concatenate([rows[i // 2] for i in range(8)], axis=1)
    delta1 = (slope1 * jnp.concatenate([wide, wide], axis=0)).astype(bf16)

    grad1 = dot_lanes(cols1, delta1).reshape(36, 8, 128)
    rows = [jnp.sum(grad1 * taps_y[q][None], axis=1) for q in range(3)]
    rows = jnp.concatenate(rows + [jnp.zeros((4, 128), f32)], axis=0)
    groups = jnp.concatenate([rows[16 * j : 16 * j + 16] for j in range(7)], axis=1)
    across[b, part:] = dot(groups.astype(bf16), table_ref[at_gather1 : at_gather1 + 896]).astype(bf16)

    total = pay[rows_of(a)].astype(f32)
    for i, copy in enumerate(parts):
        copy.wait_recv()
        total += got[i].astype(f32)
    across[b, :part] = total.astype(bf16)
    others = []
    for step in range(1, n_b):
        i, to = step - 1, in_b(step)[1]
        others.append(remote(across.at[b], across.at[b], ex_send.at[i], ex_recv.at[i], to))
        others[-1].start()
    act2 = act_sum(*halves(soft_terms(pre2)), 2).astype(bf16)
    out_ref[128:192] = dot(act2, table_ref[at_pool2 : at_pool2 + 384]).astype(bf16).astype(f32)
    for copy in parts:
        copy.wait_send()
    for copy in others:
        copy.wait()
    total = across[0].astype(f32)
    for i in range(1, n_b):
        total += across[i].astype(f32)

    full[a] = (total * (1.0 / n_dp)).astype(bf16)
    copies = []
    for step in range(1, n_a):
        i, to = step - 1, in_a(step)[1]
        copies.append(remote(full.at[a], full.at[a], ag_send.at[i], ag_recv.at[i], to))
        copies[-1].start()
    for copy in copies:
        copy.wait()
    for i in range(-(-112 // part)):
        rows = min(part, 112 - part * i)
        out_ref[part * i : part * i + rows] = full[i, :rows].astype(f32)
    total = full[0, part:].astype(f32)
    for i in range(1, n_a):
        total += full[i, part:].astype(f32)
    out_ref[112:128] = total


def unpack(in_ref, feat_hbm, g1_hbm, g2_hbm, feat_out, g1_out, g2_out, sems):
    for j in range(4):
        many = 7 if j < 3 else 6
        g2_out[7 * j : 7 * j + many] = in_ref[0 : 16 * many, 32 * j : 32 * j + 32].reshape(many, 16, 32)
    copies = [pltpu.make_async_copy(g2_out, g2_hbm, sems.at[0])]
    copies[0].start()
    for i in range(2):
        feat_out[:, i] = in_ref[128:192, 32 * i : 32 * i + 32].reshape(32, 2, 32).astype(bf16)
    copies.append(pltpu.make_async_copy(feat_out, feat_hbm, sems.at[1]))
    copies[1].start()
    for k in range(27):
        p, q, r = k // 9, k // 3 % 3, k % 3
        at = 36 * q + 4 * (3 * p + r)
        row, col = 112 + at % 16, 16 * (at // 16)
        g1_out[k] = in_ref[row : row + 4, col : col + 16]
    copies.append(pltpu.make_async_copy(g1_out, g1_hbm, sems.at[2]))
    copies[2].start()
    for copy in copies:
        copy.wait()


def shards(n_space, n_dp, volumes, first_kernel, middle_kernel, cotangent):
    n_a, n_b = 2 * n_space, n_dp // 2
    part = 16 * -(-112 // (16 * n_a))
    w1 = first_kernel.transpose(2, 3, 4, 1, 0).reshape(27, 4, 16)
    w2 = middle_kernel.transpose(2, 3, 4, 1, 0).reshape(27, 16, 32)
    cot = cotangent[0]
    vol = volumes[0]
    table = jnp.asarray(tables())
    halo = (vol.shape[0], reach) + vol.shape[2:]
    edge = (cot.shape[0],) + cot.shape[2:]
    vmem = pl.BlockSpec(memory_space=pltpu.VMEM)
    hbm = pl.BlockSpec(memory_space=pltpu.HBM)
    dma = pltpu.SemaphoreType.DMA
    packed = pl.pallas_call(
        functools.partial(kernel, n_space, n_dp, part),
        out_shape=jax.ShapeDtypeStruct((192, 128), f32),
        in_specs=[hbm] * 5,
        out_specs=vmem,
        scratch_shapes=[
            pltpu.VMEM(vol.shape, bf16),
            pltpu.VMEM(w1.shape, bf16),
            pltpu.VMEM(w2.shape, bf16),
            pltpu.VMEM(cot.shape, bf16),
            pltpu.VMEM(halo, bf16),
            pltpu.VMEM(halo, bf16),
            pltpu.VMEM(edge, bf16),
            pltpu.VMEM(edge, bf16),
            pltpu.VMEM((n_a * part, 128), bf16),
            pltpu.VMEM((n_a - 1, part, 128), bf16),
            pltpu.VMEM((n_b, part + 16, 128), bf16),
            pltpu.VMEM((n_a, part + 16, 128), bf16),
            pltpu.VMEM(table.shape, bf16),
            dma((5,)),
            dma((4,)), dma((4,)),
            dma((n_a - 1,)), dma((n_a - 1,)),
            dma((max(n_b - 1, 1),)), dma((max(n_b - 1, 1),)),
            dma((n_a - 1,)), dma((n_a - 1,)),
        ],
        compiler_params=pltpu.CompilerParams(
            collective_id=0, has_side_effects=True, vmem_limit_bytes=24 * 1024 * 1024
        ),
        cost_estimate=pl.CostEstimate(flops=400_000_000, bytes_accessed=400_000, transcendentals=1_000_000),
    )(*[pltpu.with_memory_space_constraint(x, pltpu.HBM) for x in (vol, w1, w2, cot, table)])
    features, first_grad, middle_grad = pl.pallas_call(
        unpack,
        out_shape=(
            jax.ShapeDtypeStruct(cot.shape, bf16),
            jax.ShapeDtypeStruct((27, 4, 16), f32),
            jax.ShapeDtypeStruct((27, 16, 32), f32),
        ),
        in_specs=[vmem],
        out_specs=(hbm, hbm, hbm),
        scratch_shapes=[
            pltpu.VMEM(cot.shape, bf16),
            pltpu.VMEM((27, 4, 16), f32),
            pltpu.VMEM((27, 16, 32), f32),
            dma((3,)),
        ],
        compiler_params=pltpu.CompilerParams(vmem_limit_bytes=4 * 1024 * 1024),
    )(packed)
    first_grad = first_grad.reshape(3, 3, 3, 4, 16).transpose(4, 3, 0, 1, 2)
    middle_grad = middle_grad.reshape(3, 3, 3, 16, 32).transpose(4, 3, 0, 1, 2)
    return (features[None], first_grad, middle_grad)


def solution(mesh):
    in_specs = (P("dp", None, "space", None, None), P(), P(), P("dp", None, "space", None, None))
    out_specs = (P("dp", None, "space", None, None), P(), P())
    body = functools.partial(shards, mesh.shape["space"], mesh.shape["dp"])
    return jax.shard_map(body, mesh=mesh, in_specs=in_specs, out_specs=out_specs, check_vma=False)
```
